256 devices in a mesh: tm: 8 (over x, z_lo), lat: 32 (over y, z_hi, core).
Axes of the slice: x: 4, y: 4, z: 8 (z_hi: 4, z_lo: 2; z = z_hi * 2 + z_lo), core: 2. Of those that a mesh axis runs over, the one named last changes fastest.
Arguments:
- starts: float32 [8, 3, 8, 512, 512], P('tm', None, None, 'lat'), may hold values from -1.2 to 1.2
- coarse_old: float32 [8, 3, 8, 256, 256], P('tm', None, None, 'lat'), may hold values from -1.2 to 1.2
- mean_depth: float32 [8], replicated, may hold values from 0.5 to 2
- coupling: float32 [8, 8], replicated, may hold values from 0 to 1, as said below
- wet_cells: int32 [512, 512], P('lat'), may hold values 0 or 1
Outputs:
- new_ends: float32 [8, 3, 8, 512, 512], P('tm', None, None, 'lat')
- coarse_new: float32 [8, 3, 8, 256, 256], P('tm', None, None, 'lat')
The draws below stay inside these ranges and needn't reach their ends.
Inputs may be any that keep to these rules, and one draw needn't show every extreme that they name: `coupling`: symmetric; each diagonal entry is at least 0.6 and exceeds the sum of magnitudes of the other entries of its row.
All inputs are finite; a program needn't handle non-finite values. No bound on the sum of `wet_cells` on one device may be relied on, other than what follows from the above.
Results may differ from the reference program's by a relative error of at most 0.00012.
Values sent between devices are 32-bit elements; how exact they have to be, the bound alone decides.
A program may use at most 128 MiB of HBM per device.

```python
import math
import jax
import jax.numpy as jnp
from jax import lax

LAYERS = 8
STEPS = 4
NX = 512
NY = 512
SEGMENTS = 8


def draw_coupling(key, part):
    first_key, second_key = jax.random.split(jax.random.fold_in(key, 11))
    spread = 0.5 / (LAYERS - 1)
    offside = jax.random.uniform(first_key, (LAYERS, LAYERS), jnp.float32, 0.3 * spread, spread)
    offside = 0.5 * (offside + offside.T)
    diagonal = jax.random.uniform(second_key, (LAYERS,), jnp.float32, 0.6, 1.0)
    identity = jnp.eye(LAYERS, dtype=jnp.float32)
    return offside * (1.0 - identity) + diagonal[None, :] * identity


def with_ends(values, stream_key, least, high):
    spot = [jax.random.randint(jax.random.fold_in(stream_key, axis), (), 0, length) for axis, length in enumerate(values.shape)]
    widest = values.shape.index(max(values.shape))
    beside = spot[:widest] + [(spot[widest] + 1) % values.shape[widest]] + spot[widest + 1:]
    return values.at[tuple(spot)].set(least).at[tuple(beside)].set(high)


def block_scale(stream_key, shape, cuts, least, largest):
    gain, own = 1.0, jax.random.fold_in(stream_key, 6)
    for dim, blocks in cuts:
        steps = jnp.exp(jax.random.uniform(jax.random.fold_in(own, dim), (blocks,), jnp.float32, least / len(cuts), largest / len(cuts)))
        gain = gain * jnp.repeat(steps, shape[dim] // blocks).reshape([-1 if axis == dim else 1 for axis in range(len(shape))])
    return gain


def scatter_about(rng, dims, width, limit, shards=(), kind=jnp.bfloat16):
    factor_of = block_scale(rng, dims, shards, -0.22, 0.18) if shards else 1.0
    drawn = jax.random.normal(rng, dims, jnp.float32) * width * factor_of
    return jnp.minimum(jnp.maximum(drawn, -limit), limit).astype(kind)


def setup_inputs(seed: int = 0) -> dict:
    keys = jax.random.split(jax.random.key(seed), 6)
    starts = scatter_about(keys[0], (SEGMENTS, 3, LAYERS, NY, NX), 0.3, 1.2, ((0, 8), (3, 32)), jnp.float32)
    coarse_old = scatter_about(keys[1], (SEGMENTS, 3, LAYERS, NY // 2, NX // 2), 0.3, 1.2, ((0, 8), (3, 32)), jnp.float32)
    mean_depth = jnp.clip(jnp.exp(jax.random.uniform(keys[2], (LAYERS,), jnp.float32, math.log(0.5), math.log(2.0))), 0.5, 2.0)
    coupling = draw_coupling(jax.random.fold_in(keys[5], 71), 0)
    wet_cells = with_ends((jax.random.randint(keys[4], (NY, NX), 0, 8) < 7).astype(jnp.int32), jax.random.fold_in(keys[4], 1), 0, 1)
    return {"starts": starts, "coarse_old": coarse_old, "mean_depth": mean_depth, "coupling": coupling, "wet_cells": wet_cells}


time_step = 0.15
viscosity = 0.02
rotation = 0.3


def pad_grid(field):
    field = jnp.concatenate([field[..., -1:], field, field[..., :1]], axis=-1)
    edge_rows = jnp.zeros_like(field[..., :1, :])
    return jnp.concatenate([edge_rows, field, edge_rows], axis=-2)


def gradient_east(values, spacing):
    return (values[..., 1:-1, 2:] - values[..., 1:-1, :-2]) / (2.0 * spacing)


def gradient_north(values, spacing):
    return (values[..., 2:, 1:-1] - values[..., :-2, 1:-1]) / (2.0 * spacing)


def laplacian(values, spacing):
    centre = values[..., 1:-1, 1:-1]
    beside_all = values[..., 2:, 1:-1] + values[..., :-2, 1:-1] + values[..., 1:-1, 2:] + values[..., 1:-1, :-2]
    return (beside_all - 4.0 * centre) / (spacing * spacing)


def coriolis(first_row, count, total):
    rows_here = jnp.arange(count, dtype=jnp.float32) + first_row + 0.5
    return (rotation * (2.0 * rows_here / total - 1.0))[:, None]


def tendency(padded, rotation_rows, wet_mask, mean_depth, coupling, spacing):
    height = padded[..., 0, :, :, :]
    zonal_flow = padded[..., 1, :, :, :]
    merid_flow = padded[..., 2, :, :, :]
    pressure = jnp.einsum("kj,...jrc->...krc", coupling, height, precision=lax.Precision.HIGHEST)
    thickness = mean_depth[:, None, None] + height
    zonal_mid = zonal_flow[..., 1:-1, 1:-1]
    merid_mid = merid_flow[..., 1:-1, 1:-1]
    height_rate = -(gradient_east(thickness * zonal_flow, spacing) + gradient_north(thickness * merid_flow, spacing))
    zonal_rate = -(zonal_mid * gradient_east(zonal_flow, spacing) + merid_mid * gradient_north(zonal_flow, spacing))
    zonal_rate = zonal_rate + rotation_rows * merid_mid - gradient_east(pressure, spacing) + viscosity * laplacian(zonal_flow, spacing)
    merid_rate = -(zonal_mid * gradient_east(merid_flow, spacing) + merid_mid * gradient_north(merid_flow, spacing))
    merid_rate = merid_rate - rotation_rows * zonal_mid - gradient_north(pressure, spacing) + viscosity * laplacian(merid_flow, spacing)
    return jnp.stack([height_rate, wet_mask * zonal_rate, wet_mask * merid_rate], axis=-4)


def fine_run(state, padder, rotation_rows, wet_mask, mean_depth, coupling):
    for repeat in range(STEPS):
        section_one = state + time_step * tendency(padder(state), rotation_rows, wet_mask, mean_depth, coupling, 1.0)
        section_two = 0.75 * state + 0.25 * (section_one + time_step * tendency(padder(section_one), rotation_rows, wet_mask, mean_depth, coupling, 1.0))
        state = state / 3.0 + (2.0 / 3.0) * (section_two + time_step * tendency(padder(section_two), rotation_rows, wet_mask, mean_depth, coupling, 1.0))
    return state


def coarse_step(state, padder, rotation_rows, wet_mask, mean_depth, coupling):
    return state + (STEPS * time_step) * tendency(padder(state), rotation_rows, wet_mask, mean_depth, coupling, 2.0)


def restrict(field):
    return 0.25 * (field[..., 0::2, 0::2] + field[..., 1::2, 0::2] + field[..., 0::2, 1::2] + field[..., 1::2, 1::2])


def prolong(field):
    return jnp.repeat(jnp.repeat(field, 2, axis=-2), 2, axis=-1)


def reference(starts, coarse_old, mean_depth, coupling, wet_cells):
    wet_fine = wet_cells.astype(jnp.float32)
    wet_coarse = wet_fine[0::2, 0::2] * wet_fine[1::2, 0::2] * wet_fine[0::2, 1::2] * wet_fine[1::2, 1::2]
    fine_rows = coriolis(0, NY, NY)
    coarse_rows = coriolis(0, NY // 2, NY // 2)

    def one_segment(start_state):
        return fine_run(start_state, pad_grid, fine_rows, wet_fine, mean_depth, coupling)

    fine_end = lax.map(one_segment, starts)
    delta = restrict(fine_end) - coarse_old
    first_state = restrict(starts[0])

    def link(current, correction):
        result = coarse_step(current, pad_grid, coarse_rows, wet_coarse, mean_depth, coupling)
        return correction + result, result

    unused, coarse_new = lax.scan(link, first_state, delta)
    new_ends = fine_end + prolong(coarse_new - coarse_old)
    return new_ends, coarse_new
```

```python
import functools

import jax
import jax.numpy as jnp
from jax import lax
from jax.experimental import pallas as pl
from jax.experimental.pallas import tpu as pltpu
from jax.sharding import PartitionSpec as P

MESH = pl.DeviceIdType.MESH
F32 = jnp.float32

STEPS = 4
time_step = 0.15
viscosity = 0.02
rotation = 0.3

HALO = 3


def iota(shape, dim):
    return lax.broadcasted_iota(jnp.int32, shape, dim)


def dot(a, b):
    return jnp.dot(a, b, precision=lax.Precision.HIGHEST, preferred_element_type=F32)


def rolled(x, shift):
    return pltpu.roll(x, shift % x.shape[-1], axis=x.ndim - 1)


def updated(src, r, p, depth, wet, f, spacing, old, weights, step, inside):
    k = viscosity / (spacing * spacing)
    half = 0.5 / spacing
    e, u, v = src[r, 0], src[r, 1], src[r, 2]
    un, us = src[r + 1, 1], src[r - 1, 1]
    vn, vs = src[r + 1, 2], src[r - 1, 2]
    hvn = (depth + src[r + 1, 0]) * vn
    hvs = (depth + src[r - 1, 0]) * vs
    hu = (depth + e) * u
    pc = p[r]
    ue, uw = rolled(u, -1), rolled(u, 1)
    ve, vw = rolled(v, -1), rolled(v, 1)
    u2, v2 = u * half, v * half
    east, west, north, south = k - u2, k + u2, k - v2, k + v2
    zu = (ue * east + uw * west) + (un * north + us * south)
    zv = (ve * east + vw * west) + (vn * north + vs * south)
    zu = zu + (f * v - (4.0 * k) * u) - (rolled(pc, -1) - rolled(pc, 1))
    zv = zv - (f * u + (4.0 * k) * v) - (p[r + 1] - p[r - 1])
    ze = (rolled(hu, -1) - rolled(hu, 1)) + (hvn - hvs)
    w = wet * step
    ce = jnp.where(inside, -step * half, 0.0).astype(F32)
    out = [ce * ze, w * zu, w * zv]
    first, second = weights
    now = [e, u, v]
    for i in range(3):
        out[i] = out[i] + (now[i] if second == 1.0 else second * now[i])
        if first != 0.0:
            out[i] = out[i] + first * old[r, i]
    return out


def kernel(NT, NL, starts, coarse_old, mean_depth, coupling, wet_cells, ends, coarse_new,
           YA, Y1, Y2, PB, WET, WX, HB, KF, KC, WW, W2, WR, WP, DL, TX, RX, TC, RC, CT, PC, WC, RES,
           CO, BW, CN, C0, P0, W0,
           hs_send, hs_recv, wx_send, wx_recv, tx_send, rx_recv, tc_send, rc_recv):
    R, W = wet_cells.shape
    L = 8
    RC_ROWS, WCO = R // 2, W // 2
    SLAB = WCO // NT
    n, q = lax.axis_index("tm"), lax.axis_index("lat")
    up, down = q > 0, q < NL - 1
    inside_side = {-1: up, 1: down}

    barrier = pltpu.get_barrier_semaphore()

    def greet(m, row):
        pl.semaphore_signal(barrier, inc=1, device_id=(m, row), device_id_type=MESH)

    for j in range(1, NT):
        greet(lax.rem(n + j, NT), q)
    for d in (-1, 1):
        @pl.when(inside_side[d])
        def _(d=d):
            for j in range(NT):
                greet(lax.rem(n + j, NT), q + d)

    for f in range(3):
        for b in range(R // 8):
            YA[pl.ds(HALO + 8 * b, 8), f] = jnp.swapaxes(starts[f, :, pl.ds(8 * b, 8), :], 0, 1)

    pl.semaphore_wait(barrier, (NT - 1) + NT * up.astype(jnp.int32) + NT * down.astype(jnp.int32))

    def halo_copy(k, side):
        first = HALO if side == -1 else R
        slot = 1 if side == -1 else 0
        return pltpu.make_async_remote_copy(
            src_ref=YA.at[pl.ds(first, HALO)], dst_ref=HB.at[k, slot],
            send_sem=hs_send.at[k, slot], recv_sem=hs_recv.at[k, slot],
            device_id=(n, q + side), device_id_type=MESH)

    def halo_arrival(k, slot, side):
        return pltpu.make_async_remote_copy(
            src_ref=YA.at[pl.ds(0, HALO)], dst_ref=HB.at[k, slot],
            send_sem=hs_send.at[k, slot], recv_sem=hs_recv.at[k, slot],
            device_id=(n, q + side), device_id_type=MESH)

    def wet_copy(side):
        slot = 1 if side == -1 else 0
        return pltpu.make_async_remote_copy(
            src_ref=wet_cells, dst_ref=WX.at[slot], send_sem=wx_send.at[slot], recv_sem=wx_recv.at[slot],
            device_id=(n, q + side), device_id_type=MESH)

    def send_halos(k):
        for side in (-1, 1):
            @pl.when(inside_side[side])
            def _(side=side):
                halo_copy(k, side).start()

    send_halos(0)
    for side in (-1, 1):
        @pl.when(inside_side[side])
        def _(side=side):
            wet_copy(side).start()

        @pl.when(jnp.logical_not(inside_side[side]))
        def _(side=side):
            slot = 0 if side == -1 else 1
            WX[slot] = jnp.zeros((R, W), jnp.int32)
            YA[pl.ds(0 if side == -1 else HALO + R, HALO)] = jnp.zeros((HALO, 3, L, W), F32)
            RX[:, pl.ds(0 if side == -1 else RC_ROWS, RC_ROWS // 2)] = jnp.zeros(
                (NT - 1, RC_ROWS // 2, 3, L, 128), F32)

    KN = KF.shape[0]
    spread = (iota((KN, L), 0) % L == iota((KN, L), 1)).astype(F32)
    spread_t = (iota((L, KN), 1) % L == iota((L, KN), 0)).astype(F32)
    blocks = dot(dot(spread, coupling[...]), spread_t)
    blocks = jnp.where(iota((KN, KN), 0) // L == iota((KN, KN), 1) // L, blocks, 0.0)
    KF[...] = 0.5 * blocks
    KC[...] = 0.25 * blocks

    def depth_of(width):
        rows = iota((L, width), 0)
        value = jnp.zeros((L, width), F32)
        for l in range(L):
            value = jnp.where(rows == l, mean_depth[l], value)
        return value

    wet_own = wet_cells[...].astype(F32)
    for r in range(R):
        WET[HALO + r] = jnp.broadcast_to(wet_own[r:r + 1, :], (L, W))

    target = (iota((W, W), 1) // 64 * SLAB - 16 + iota((W, W), 1) % 64 + WCO) % WCO
    WW[...] = (iota((W, W), 0) // 2 == target).astype(F32)
    W2[...] = (iota((WCO, W), 0) == target[:WCO]).astype(F32)
    WR[...] = (iota((W, WCO), 0) // 2 == iota((W, WCO), 1)).astype(F32)
    WP[...] = (iota((WCO, W), 1) // 2 == iota((WCO, W), 0)).astype(F32)

    @pl.when(n == 0)
    def _():
        sums = jnp.stack([YA[HALO + 2 * i] + YA[HALO + 1 + 2 * i] for i in range(RC_ROWS)])
        C0[pl.ds(1, RC_ROWS)] = (0.25 * dot(sums.reshape(-1, W), WR[...])).reshape(RC_ROWS, 3, L, WCO)

    for f in range(3):
        CO[:, f] = jnp.swapaxes(coarse_old[f], 0, 1)

    def fine_f(r):
        row = q * R + (r - HALO)
        return rotation * (2.0 * (row.astype(F32) + 0.5) / (R * NL) - 1.0), (row >= 0) & (row < R * NL)

    stages = (
        (YA, Y1, (0.0, 1.0), 1.0),
        (Y1, Y2, (0.75, 0.25), 0.25),
        (Y2, YA, (1.0 / 3.0, 2.0 / 3.0), 2.0 / 3.0),
    )

    def pressure(stage, pieces):
        src = stages[stage][0]
        count = sum(c for _, c in pieces)
        rows = [src[pl.ds(a, c), 0] for a, c in pieces]
        rows = rows[0] if len(rows) == 1 else jnp.concatenate(rows, axis=0)
        size = count * L
        result = dot(KF[pl.ds(0, size), pl.ds(0, size)], rows.reshape(size, W)).reshape(count, L, W)
        at = 0
        for a, c in pieces:
            PB[stage, pl.ds(a, c)] = result[at:at + c]
            at += c

    def fine_row(stage, r):
        src, dst, weights, g = stages[stage]
        f, inside = fine_f(r)
        new = updated(src, r, PB.at[stage], depth_of(W), WET[r], f, 1.0, YA, weights, g * time_step, inside)
        for i in range(3):
            dst[r, i] = new[i]

    def coarse_first():
        sums = jnp.stack([YA[1] + YA[2], YA[HALO + R] + YA[HALO + R + 1]])
        outer = (0.25 * dot(sums.reshape(-1, W), WR[...])).reshape(2, 3, L, WCO)
        C0[0] = outer[0]
        C0[RC_ROWS + 1] = outer[1]
        size = (RC_ROWS + 2) * L
        P0[...] = dot(KC[pl.ds(0, size), pl.ds(0, size)], C0[:, 0].reshape(size, WCO)).reshape(RC_ROWS + 2, L, WCO)
        pairs = (iota((RC_ROWS, R), 1) // 2 == iota((RC_ROWS, R), 0)).astype(F32)
        wet_full = (dot(dot(pairs, wet_cells[...].astype(F32)), WR[...]) > 3.5).astype(F32)
        for i in range(RC_ROWS):
            W0[i] = jnp.broadcast_to(wet_full[i:i + 1, :], (L, WCO))

        @pl.loop(1, RC_ROWS + 1)
        def _(r):
            row = q * RC_ROWS + r - 1
            f = rotation * (2.0 * (row.astype(F32) + 0.5) / (RC_ROWS * NL) - 1.0)
            new = updated(C0, r, P0, depth_of(WCO), W0[r - 1], f, 2.0, None, (0.0, 1.0), STEPS * time_step, True)
            for i in range(3):
                CN[r - 1, i] = new[i]

    @pl.loop(0, STEPS)
    def _(k):
        for stage in range(3):
            pressure(stage, [(HALO + stage, R - 2 * stage)])

            @pl.loop(0, (R - 2 * (stage + 1)) // 2)
            def _(j, stage=stage):
                for more in range(2):
                    fine_row(stage, HALO + stage + 1 + 2 * j + more)

        for side in (-1, 1):
            slot = 0 if side == -1 else 1

            @pl.when(inside_side[side])
            def _(side=side, slot=slot):
                halo_arrival(k, slot, side).wait_recv()
                YA[pl.ds(0 if side == -1 else HALO + R, HALO)] = HB[k, slot]
                halo_copy(k, side).wait_send()

        @pl.when(k == 0)
        def _():
            for side in (-1, 1):
                @pl.when(inside_side[side])
                def _(side=side):
                    wet_copy(side).wait_send()
                    wet_copy(-side).wait_recv()
            for r in range(HALO):
                WET[r] = jnp.broadcast_to(WX[0, R - HALO + r:R - HALO + r + 1, :].astype(F32), (L, W))
                WET[HALO + R + r] = jnp.broadcast_to(WX[1, r:r + 1, :].astype(F32), (L, W))

            @pl.when(n == 0)
            def _():
                coarse_first()
                BW[...] = dot((CN[...] - CO[...]).reshape(-1, WCO), W2[...])

            @pl.when(n > 0)
            def _():
                BW[...] = dot((-CO[...]).reshape(-1, WCO), W2[...])

        for stage in range(3):
            pressure(stage, [(stage, HALO), (HALO + R - stage, HALO)])

            @pl.loop(0, HALO)
            def _(j, stage=stage):
                fine_row(stage, stage + 1 + j)
                fine_row(stage, R - stage + 2 + j)

        @pl.when(k < STEPS - 1)
        def _():
            send_halos(k + 1)

    sums = jnp.stack([YA[HALO + 2 * i] + YA[HALO + 1 + 2 * i] for i in range(RC_ROWS)])
    DL[...] = (0.25 * dot(sums.reshape(-1, W), WW[...]) + BW[...]).reshape(RC_ROWS, 3, L, W)
    lanes = iota((L, 128), 1)
    for i in range(RC_ROWS // 2):
        for f in range(3):
            for j in range(NT // 2):
                a = DL[2 * i, f, :, pl.ds(128 * j, 128)]
                b = DL[2 * i + 1, f, :, pl.ds(128 * j, 128)]
                TX[2 * j, i, f] = jnp.where(lanes < 64, a, rolled(b, 64))
                TX[2 * j + 1, i, f] = jnp.where(lanes < 64, rolled(a, 64), b)

    HU = RC_ROWS // 2

    def delta_copy(m, d, units):
        first, to = {0: (0, HU), 1: (HU - units, HU - units), -1: (0, 2 * HU)}[d]
        return pltpu.make_async_remote_copy(
            src_ref=TX.at[m, pl.ds(first, units)], dst_ref=RX.at[n, pl.ds(to, units)],
            send_sem=tx_send.at[m, d + 1], recv_sem=rx_recv.at[n, d + 1],
            device_id=(m, q + d), device_id_type=MESH)

    def delta_arrival(s, d, units):
        to = {0: HU, 1: HU - units, -1: 2 * HU}[d]
        return pltpu.make_async_remote_copy(
            src_ref=TX.at[0, pl.ds(0, units)], dst_ref=RX.at[s, pl.ds(to, units)],
            send_sem=tx_send.at[0, d + 1], recv_sem=rx_recv.at[s, d + 1],
            device_id=(s, q - d), device_id_type=MESH)

    def for_deltas(act):
        for units in sorted({(NT - s) // 2 for s in range(NT - 1)}):
            @pl.when((n < NT - 1) & ((NT - n) // 2 == units))
            def _(units=units):
                @pl.loop(0, NT)
                def _(j):
                    m = lax.rem(n + j, NT)

                    @pl.when(down)
                    def _():
                        act(delta_copy(m, 1, units))

                    @pl.when(up)
                    def _():
                        act(delta_copy(m, -1, units))

                    @pl.when(j > 0)
                    def _():
                        act(delta_copy(m, 0, HU))

    for_deltas(lambda copy: copy.start())

    @pl.when(n < NT - 1)
    def _():
        RX[n, pl.ds(HU, HU)] = TX[n]

    E = 3 * RC_ROWS
    col = iota((W, 128), 1)
    own = (n * SLAB - 16 + col + WCO) % WCO
    picks = jnp.where((iota((W, 128), 0) // 2 == own) & (col < 64), 1.0, 0.0).astype(F32)
    pairs = (iota((RC_ROWS, R), 1) // 2 == iota((RC_ROWS, R), 0)).astype(F32)
    for part, cells in enumerate((WX[0], wet_cells[...], WX[1])):
        window = (dot(dot(pairs, cells.astype(F32)), picks) > 3.5).astype(F32)
        for i in range(RC_ROWS):
            WC[part * RC_ROWS + i] = jnp.broadcast_to(window[i:i + 1, :], (L, 128))

    def arrived(s):
        h = (NT - s) // 2

        @pl.when(up)
        def _():
            delta_arrival(s, 1, h).wait_recv()

        @pl.when(down)
        def _():
            delta_arrival(s, -1, h).wait_recv()

        @pl.when(n != s)
        def _():
            delta_arrival(s, 0, HU).wait_recv()

    def row_of(s, r, f):
        x = RX[s, r // 2, f]
        return x if r % 2 == 0 else rolled(x, 64)

    arrived(0)
    for r in range(E):
        for f in range(3):
            CT[0, r, f] = row_of(0, r, f)

    def result_copy(s):
        return pltpu.make_async_remote_copy(
            src_ref=TC.at[s], dst_ref=RC.at[n], send_sem=tc_send.at[s], recv_sem=rc_recv.at[n],
            device_id=(s, q), device_id_type=MESH)

    def result_arrival(m):
        return pltpu.make_async_remote_copy(
            src_ref=TC.at[0], dst_ref=RC.at[m], send_sem=tc_send.at[0], recv_sem=rc_recv.at[m],
            device_id=(m, q), device_id_type=MESH)

    depth = depth_of(128)
    group = lanes // SLAB
    for s in range(1, NT):
        now, later = CT.at[(s - 1) % 2], CT.at[s % 2]
        h = NT - 1 - s
        lo, hi = RC_ROWS - h, 2 * RC_ROWS + h
        size = (hi - lo + 2) * L
        PC[pl.ds(lo - 1, hi - lo + 2)] = dot(
            KC[pl.ds(0, size), pl.ds(0, size)], now[pl.ds(lo - 1, hi - lo + 2), 0].reshape(size, 128)
        ).reshape(hi - lo + 2, L, 128)
        if s < NT - 1:
            arrived(s)
        for r in range(lo, hi):
            row = q * RC_ROWS + (r - RC_ROWS)
            f = rotation * (2.0 * (row.astype(F32) + 0.5) / (RC_ROWS * NL) - 1.0)
            inside = (row >= 0) & (row < RC_ROWS * NL)
            new = updated(now, r, PC, depth, WC[r], f, 2.0, None, (0.0, 1.0), STEPS * time_step, inside)
            for i in range(3):
                if RC_ROWS <= r < 2 * RC_ROWS:
                    RES[r - RC_ROWS, i] = new[i]
                if s < NT - 1:
                    later[r, i] = new[i] + row_of(s, r, i)
        for b in range(2):
            for i in range(3):
                packed = rolled(RES[4 * b, i], -16)
                for g in range(1, 4):
                    packed = jnp.where(group == g, rolled(RES[4 * b + g, i], SLAB * g - 16), packed)
                TC[s, b, i] = packed

        @pl.when(n != s)
        def _(s=s):
            result_copy(s).start()

        @pl.when(n == s)
        def _(s=s):
            RC[s] = TC[s]

    @pl.when(n > 0)
    def _():
        @pl.loop(1, NT)
        def _(j):
            result_arrival(lax.rem(n + j, NT)).wait_recv()

        for r in range(RC_ROWS):
            b, g = r // 4, r % 4
            for i in range(3):
                for j in range(WCO // 128):
                    value = rolled(RC[4 * j, b, i], -SLAB * g)
                    for m in range(1, 4):
                        value = jnp.where(group == m, rolled(RC[4 * j + m, b, i], SLAB * (m - g)), value)
                    CN[r, i, :, pl.ds(128 * j, 128)] = value

    change = dot((CN[...] - CO[...]).reshape(-1, WCO), WP[...]).reshape(RC_ROWS, 3, L, W)
    for i in range(3):
        coarse_new[i] = jnp.swapaxes(CN[:, i], 0, 1)
    for r in range(RC_ROWS):
        for i in range(3):
            for more in range(2):
                YA[HALO + 2 * r + more, i] = YA[HALO + 2 * r + more, i] + change[r, i]
    for i in range(3):
        for b in range(R // 8):
            ends[i, :, pl.ds(8 * b, 8), :] = jnp.swapaxes(YA[pl.ds(HALO + 8 * b, 8), i], 0, 1)

    for_deltas(lambda copy: copy.wait_send())
    for s in range(1, NT):
        @pl.when(n != s)
        def _(s=s):
            result_copy(s).wait_send()


def local(NT, NL, starts, coarse_old, mean_depth, coupling, wet_cells):
    R, W = wet_cells.shape
    L = 8
    C, WCO = R // 2, W // 2
    E = R + 2 * HALO
    vmem = lambda *shape: pltpu.VMEM(shape, F32)
    sems = lambda *shape: pltpu.SemaphoreType.DMA(shape)
    space = pl.BlockSpec(memory_space=pltpu.VMEM)
    ends, coarse_new = pl.pallas_call(
        functools.partial(kernel, NT, NL),
        out_shape=(jax.ShapeDtypeStruct((3, L, R, W), F32), jax.ShapeDtypeStruct((3, L, C, WCO), F32)),
        in_specs=[space, space, pl.BlockSpec(memory_space=pltpu.SMEM), space, space],
        out_specs=(space, space),
        scratch_shapes=[
            vmem(E, 3, L, W), vmem(E, 3, L, W), vmem(E, 3, L, W), vmem(3, E, L, W), vmem(E, L, W),
            pltpu.VMEM((2, R, W), jnp.int32), vmem(STEPS, 2, HALO, 3, L, W),
            vmem(3 * C * L, 3 * C * L), vmem(3 * C * L, 3 * C * L),
            vmem(W, W), vmem(WCO, W), vmem(W, WCO), vmem(WCO, W), vmem(C, 3, L, W),
            vmem(NT, C // 2, 3, L, 128), vmem(NT - 1, 3 * C // 2, 3, L, 128),
            vmem(NT, 2, 3, L, 128), vmem(NT, 2, 3, L, 128),
            vmem(2, 3 * C, 3, L, 128), vmem(3 * C, L, 128), vmem(3 * C, L, 128), vmem(C, 3, L, 128),
            vmem(C, 3, L, WCO), vmem(C * 3 * L, W), vmem(C, 3, L, WCO),
            vmem(C + 2, 3, L, WCO), vmem(C + 2, L, WCO), vmem(C, L, WCO),
            sems(STEPS, 2), sems(STEPS, 2), sems(2), sems(2), sems(NT, 3), sems(NT - 1, 3), sems(NT), sems(NT),
        ],
        compiler_params=pltpu.CompilerParams(
            collective_id=0, has_side_effects=True, vmem_limit_bytes=48 * 1024 * 1024),
    )(starts[0], coarse_old[0], mean_depth, coupling, wet_cells)
    return ends[None], coarse_new[None]


def solution(mesh):
    NT, NL = mesh.shape["tm"], mesh.shape["lat"]
    in_specs = (
        P("tm", None, None, "lat", None),
        P("tm", None, None, "lat", None),
        P(),
        P(),
        P("lat", None),
    )
    out_specs = (P("tm", None, None, "lat", None), P("tm", None, None, "lat", None))
    return jax.shard_map(functools.partial(local, NT, NL), mesh=mesh, in_specs=in_specs, out_specs=out_specs,
                         check_vma=False)
```

```python
import functools

import jax
import jax.numpy as jnp
from jax import lax
from jax.experimental import pallas as pl
from jax.experimental.pallas import tpu as pltpu
from jax.sharding import PartitionSpec as P

MESH = pl.DeviceIdType.MESH
F32 = jnp.float32

STEPS = 4
time_step = 0.15
viscosity = 0.02
rotation = 0.3

HALO = 3


def iota(shape, dim):
    return lax.broadcasted_iota(jnp.int32, shape, dim)


def dot(a, b):
    return jnp.dot(a, b, precision=lax.Precision.HIGHEST, preferred_element_type=F32)


def split(x, terms):
    parts = []
    for _ in range(terms):
        part = x.astype(jnp.bfloat16)
        parts.append(part)
        x = x - part.astype(F32)
    return parts


def picked(x, selector):
    selector = selector.astype(jnp.bfloat16)
    high, middle, low = [jnp.dot(part, selector, preferred_element_type=F32) for part in split(x, 3)]
    return high + (middle + low)


def mixed(matrix, x):
    high, low = split(matrix, 2)
    x_high, x_low = split(x, 2)
    product = lambda a, b: jnp.dot(a, b, preferred_element_type=F32)
    return product(high, x_high) + (product(high, x_low) + product(low, x_high))


def widened(x, width):
    return x if width == x.shape[1] else jnp.concatenate([x] * (width // x.shape[1]), axis=1)


def rolled(x, shift):
    return pltpu.roll(x, shift % x.shape[-1], axis=x.ndim - 1)


def updated(src, r, p, depth, wet, f, spacing, old, weights, step, inside):
    k = viscosity / (spacing * spacing)
    half = 0.5 / spacing
    e, u, v = src[r, 0], src[r, 1], src[r, 2]
    un, us = src[r + 1, 1], src[r - 1, 1]
    vn, vs = src[r + 1, 2], src[r - 1, 2]
    hvn = (depth + src[r + 1, 0]) * vn
    hvs = (depth + src[r - 1, 0]) * vs
    hu = (depth + e) * u
    pc = p[r]
    ue, uw = rolled(u, -1), rolled(u, 1)
    ve, vw = rolled(v, -1), rolled(v, 1)
    u2, v2 = u * half, v * half
    east, west, north, south = k - u2, k + u2, k - v2, k + v2
    zu = (ue * east + uw * west) + (un * north + us * south)
    zv = (ve * east + vw * west) + (vn * north + vs * south)
    zu = zu + (f * v - (4.0 * k) * u) - (rolled(pc, -1) - rolled(pc, 1))
    zv = zv - (f * u + (4.0 * k) * v) - (p[r + 1] - p[r - 1])
    ze = (rolled(hu, -1) - rolled(hu, 1)) + (hvn - hvs)
    w = wet * step
    ce = jnp.where(inside, -step * half, 0.0).astype(F32)
    out = [ce * ze, w * zu, w * zv]
    first, second = weights
    now = [e, u, v]
    for i in range(3):
        out[i] = out[i] + (now[i] if second == 1.0 else second * now[i])
        if first != 0.0:
            out[i] = out[i] + first * old[r, i]
    return out


def kernel(NT, NL, starts_in, old_in, depth_in, coupling_in, wet_in, ends, coarse_new,
           SV, OV, CV, WV, DS, DP, CF, in_sem, YA, Y1, Y2, PB, WET, WX, HB, KF, KC, WW, W2, WR, WP, DL, TX, RX, TC, RC, CT, PC, WC, RES,
           CO, BW, CN, C0, P0, W0,
           hs_send, hs_recv, wx_send, wx_recv, tx_send, rx_recv, tc_send, rc_recv):
    starts, coarse_old, mean_depth, coupling, wet_cells = SV, OV, DS, CV, WV
    R, W = wet_cells.shape
    L = 8
    fetches = [pltpu.make_async_copy(source, target, in_sem.at[i]) for i, (source, target) in enumerate(
        ((starts_in, SV), (wet_in, WV), (coupling_in, CV), (depth_in, DS), (old_in, OV)))]
    for fetch in fetches:
        fetch.start()
    RC_ROWS, WCO = R // 2, W // 2
    SLAB = WCO // NT
    n, q = lax.axis_index("tm"), lax.axis_index("lat")
    up, down = q > 0, q < NL - 1
    inside_side = {-1: up, 1: down}

    barrier = pltpu.get_barrier_semaphore()

    def greet(m, row):
        pl.semaphore_signal(barrier, inc=1, device_id=(m, row), device_id_type=MESH)

    for j in range(1, NT):
        greet(lax.rem(n + j, NT), q)
    for d in (-1, 1):
        @pl.when(inside_side[d])
        def _(d=d):
            for j in range(NT):
                greet(lax.rem(n + j, NT), q + d)

    fetches[0].wait()
    for f in range(3):
        for b in range(R // 8):
            YA[pl.ds(HALO + 8 * b, 8), f] = jnp.swapaxes(starts[f, :, pl.ds(8 * b, 8), :], 0, 1)

    pl.semaphore_wait(barrier, (NT - 1) + NT * up.astype(jnp.int32) + NT * down.astype(jnp.int32))

    def halo_copy(k, side, j):
        row = HALO + HALO - 1 - j if side == -1 else R + j
        slot = 1 if side == -1 else 0
        return pltpu.make_async_remote_copy(
            src_ref=YA.at[row], dst_ref=HB.at[k, slot, row - HALO if side == -1 else j],
            send_sem=hs_send.at[k, slot, j], recv_sem=hs_recv.at[k, slot, j],
            device_id=(n, q + side), device_id_type=MESH)

    def halo_arrival(k, side, j):
        slot = 0 if side == -1 else 1
        return pltpu.make_async_remote_copy(
            src_ref=YA.at[0], dst_ref=HB.at[k, slot, j if side == -1 else HALO - 1 - j],
            send_sem=hs_send.at[k, slot, j], recv_sem=hs_recv.at[k, slot, j],
            device_id=(n, q + side), device_id_type=MESH)

    def wet_copy(side):
        slot = 1 if side == -1 else 0
        return pltpu.make_async_remote_copy(
            src_ref=wet_cells, dst_ref=WX.at[slot], send_sem=wx_send.at[slot], recv_sem=wx_recv.at[slot],
            device_id=(n, q + side), device_id_type=MESH)

    def send_row(k, j):
        for side in (-1, 1):
            @pl.when(inside_side[side])
            def _(side=side):
                halo_copy(k, side, j).start()

    for j in range(HALO):
        send_row(0, j)
    for fetch in fetches[1:]:
        fetch.wait()
    for side in (-1, 1):
        @pl.when(inside_side[side])
        def _(side=side):
            wet_copy(side).start()

        @pl.when(jnp.logical_not(inside_side[side]))
        def _(side=side):
            slot = 0 if side == -1 else 1
            WX[slot] = jnp.zeros((R, W), jnp.int32)
            YA[pl.ds(0 if side == -1 else HALO + R, HALO)] = jnp.zeros((HALO, 3, L, W), F32)
            RX[:, pl.ds(0 if side == -1 else RC_ROWS, RC_ROWS // 2)] = jnp.zeros(
                (NT - 1, RC_ROWS // 2, 3, L, 128), F32)

    KN = KF.shape[0]
    spread = (iota((KN, L), 0) % L == iota((KN, L), 1)).astype(F32)
    spread_t = (iota((L, KN), 1) % L == iota((L, KN), 0)).astype(F32)
    blocks = dot(dot(spread, coupling[...]), spread_t)
    blocks = jnp.where(iota((KN, KN), 0) // L == iota((KN, KN), 1) // L, blocks, 0.0)
    KF[...] = 0.5 * blocks
    KC[...] = 0.25 * blocks
    for shift in range(L):
        column = (iota((L, L), 0) - shift + L) & (L - 1)
        part = jnp.sum(jnp.where(iota((L, L), 1) == column, coupling[...], 0.0), axis=1, keepdims=True)
        CF[shift] = jnp.broadcast_to(0.5 * part, (L, 128))

    layer = iota((L, 128), 0)
    value = jnp.zeros((L, 128), F32)
    for l in range(L):
        value = jnp.where(layer == l, mean_depth[l], value)
    DP[...] = value

    def depth_of(width):
        return widened(DP[...], width)

    wet_own = wet_cells[...].astype(F32)
    for r in range(R):
        WET[HALO + r] = jnp.broadcast_to(wet_own[r:r + 1, :], (L, W))

    position = iota((8, W), 1)
    target = ((position >> 6) * SLAB - 16 + (position & 63)) & (WCO - 1)
    target = target[:1]
    WW[...] = ((iota((W, W), 0) >> 1) == target).astype(F32)
    W2[...] = (iota((WCO, W), 0) == target).astype(F32)
    WR[...] = ((iota((W, WCO), 0) >> 1) == iota((W, WCO), 1)).astype(F32)
    WP[...] = ((iota((WCO, W), 1) >> 1) == iota((WCO, W), 0)).astype(F32)

    @pl.when(n == 0)
    def _():
        sums = jnp.stack([YA[HALO + 2 * i] + YA[HALO + 1 + 2 * i] for i in range(RC_ROWS)])
        C0[pl.ds(1, RC_ROWS)] = (0.25 * picked(sums.reshape(-1, W), WR[...])).reshape(RC_ROWS, 3, L, WCO)

    for f in range(3):
        CO[:, f] = jnp.swapaxes(coarse_old[f], 0, 1)

    def fine_f(r):
        row = q * R + (r - HALO)
        return rotation * (2.0 * (row.astype(F32) + 0.5) / (R * NL) - 1.0), (row >= 0) & (row < R * NL)

    stages = (
        (YA, Y1, (0.0, 1.0), 1.0),
        (Y1, Y2, (0.75, 0.25), 0.25),
        (Y2, YA, (1.0 / 3.0, 2.0 / 3.0), 2.0 / 3.0),
    )

    def pressure(stage, pieces):
        src = stages[stage][0]
        count = sum(c for _, c in pieces)
        rows = [src[pl.ds(a, c), 0] for a, c in pieces]
        rows = rows[0] if len(rows) == 1 else jnp.concatenate(rows, axis=0)
        size = count * L
        result = mixed(KF[pl.ds(0, size), pl.ds(0, size)], rows.reshape(size, W)).reshape(count, L, W)
        at = 0
        for a, c in pieces:
            PB[stage, pl.ds(a, c)] = result[at:at + c]
            at += c

    def row_pressure(stage, r):
        e = stages[stage][0][r, 0]
        total = widened(CF[0], W) * e
        for shift in range(1, L):
            total = total + widened(CF[shift], W) * pltpu.roll(e, shift, axis=0)
        PB[stage, r] = total

    def fine_row(stage, r):
        src, dst, weights, g = stages[stage]
        f, inside = fine_f(r)
        new = updated(src, r, PB.at[stage], depth_of(W), WET[r], f, 1.0, YA, weights, g * time_step, inside)
        for i in range(3):
            dst[r, i] = new[i]

    def coarse_first():
        sums = jnp.stack([YA[1] + YA[2], YA[HALO + R] + YA[HALO + R + 1]])
        outer = (0.25 * picked(sums.reshape(-1, W), WR[...])).reshape(2, 3, L, WCO)
        C0[0] = outer[0]
        C0[RC_ROWS + 1] = outer[1]
        size = (RC_ROWS + 2) * L
        P0[...] = mixed(KC[pl.ds(0, size), pl.ds(0, size)], C0[:, 0].reshape(size, WCO)).reshape(RC_ROWS + 2, L, WCO)
        pairs = (iota((RC_ROWS, R), 1) // 2 == iota((RC_ROWS, R), 0)).astype(F32)
        wet_full = (jnp.dot(jnp.dot(pairs, wet_cells[...].astype(F32)), WR[...]) > 3.5).astype(F32)
        for i in range(RC_ROWS):
            W0[i] = jnp.broadcast_to(wet_full[i:i + 1, :], (L, WCO))

        @pl.loop(1, RC_ROWS + 1)
        def _(r):
            row = q * RC_ROWS + r - 1
            f = rotation * (2.0 * (row.astype(F32) + 0.5) / (RC_ROWS * NL) - 1.0)
            new = updated(C0, r, P0, depth_of(WCO), W0[r - 1], f, 2.0, None, (0.0, 1.0), STEPS * time_step, True)
            for i in range(3):
                CN[r - 1, i] = new[i]

    HU = RC_ROWS // 2
    lanes = iota((L, 128), 1)

    def slot_of(unit):
        return {1: 0, 2: 1, 0: 2, 3: 3}[unit]

    def deltas(first, last):
        rows = range(2 * first, 2 * last)
        count = len(rows)
        sums = jnp.stack([YA[HALO + 2 * i] + YA[HALO + 1 + 2 * i] for i in rows])
        bias = BW[pl.ds(2 * first * 3 * L, count * 3 * L)]
        DL[pl.ds(2 * first, count)] = (0.25 * picked(sums.reshape(-1, W), WW[...]) + bias).reshape(count, 3, L, W)
        for i in range(first, last):
            for f in range(3):
                for j in range(NT // 2):
                    a = DL[2 * i, f, :, pl.ds(128 * j, 128)]
                    b = DL[2 * i + 1, f, :, pl.ds(128 * j, 128)]
                    TX[2 * j, slot_of(i), f] = jnp.where(lanes < 64, a, rolled(b, 64))
                    TX[2 * j + 1, slot_of(i), f] = jnp.where(lanes < 64, rolled(a, 64), b)

    def piece(d, phase, units):
        if d == 0 or units == 4:
            return 2 * phase, 2
        if phase == 1:
            return (3 if d == 1 else 2), 1
        return {1: (0, 0), 2: (1 if d == 1 else 0, 1), 3: (0, 2)}[units]

    def delta_copy(m, d, phase, units):
        first, count = piece(d, phase, units)
        return pltpu.make_async_remote_copy(
            src_ref=TX.at[m, pl.ds(first, count)], dst_ref=RX.at[n, pl.ds(HU * (1 - d) + first, count)],
            send_sem=tx_send.at[m, d + 1, phase], recv_sem=rx_recv.at[n, d + 1, phase],
            device_id=(m, q + d), device_id_type=MESH)

    def delta_arrival(s, d, phase, units):
        first, count = piece(d, phase, units)
        return pltpu.make_async_remote_copy(
            src_ref=TX.at[0, pl.ds(first, count)], dst_ref=RX.at[s, pl.ds(HU * (1 - d) + first, count)],
            send_sem=tx_send.at[0, d + 1, phase], recv_sem=rx_recv.at[s, d + 1, phase],
            device_id=(s, q - d), device_id_type=MESH)

    def for_deltas(phase, act):
        for units in sorted({(NT - s) // 2 for s in range(NT - 1)}):
            @pl.when((n < NT - 1) & ((NT - n) // 2 == units))
            def _(units=units):
                @pl.loop(0, NT)
                def _(j):
                    m = lax.rem(n + j, NT)
                    for d, there in ((1, down), (-1, up), (0, j > 0)):
                        if piece(d, phase, units)[1]:
                            @pl.when(there)
                            def _(d=d):
                                act(delta_copy(m, d, phase, units))

    @pl.loop(0, STEPS)
    def _(k):
        for stage in range(3):
            pressure(stage, [(HALO + stage, R - 2 * stage)])

            @pl.loop(0, (R - 2 * (stage + 1)) // 2)
            def _(j, stage=stage):
                for more in range(2):
                    fine_row(stage, HALO + stage + 1 + 2 * j + more)

        @pl.when(k == STEPS - 1)
        def _():
            deltas(1, 3)
            for_deltas(0, lambda copy: copy.start())

        for side in (-1, 1):
            slot = 0 if side == -1 else 1

            @pl.when(inside_side[side])
            def _(side=side, slot=slot):
                for j in range(HALO):
                    halo_arrival(k, side, j).wait_recv()
                YA[pl.ds(0 if side == -1 else HALO + R, HALO)] = HB[k, slot]
                for j in range(HALO):
                    halo_copy(k, side, j).wait_send()

        @pl.when(k == 0)
        def _():
            for side in (-1, 1):
                @pl.when(inside_side[side])
                def _(side=side):
                    wet_copy(side).wait_send()
                    wet_copy(-side).wait_recv()
            for r in range(HALO):
                WET[r] = jnp.broadcast_to(WX[0, R - HALO + r:R - HALO + r + 1, :].astype(F32), (L, W))
                WET[HALO + R + r] = jnp.broadcast_to(WX[1, r:r + 1, :].astype(F32), (L, W))

        for j in range(HALO):
            for stage in range(3):
                low, high = HALO - j + stage, HALO + R - 1 + j - stage
                row_pressure(stage, low - 1)
                row_pressure(stage, high + 1)
                fine_row(stage, low)
                fine_row(stage, high)

            @pl.when(k < STEPS - 1)
            def _(j=j):
                send_row(k + 1, j)

        @pl.when(k == 0)
        def _():
            @pl.when(n == 0)
            def _():
                coarse_first()
                BW[...] = picked((CN[...] - CO[...]).reshape(-1, WCO), W2[...])

            @pl.when(n > 0)
            def _():
                BW[...] = picked((-CO[...]).reshape(-1, WCO), W2[...])

    deltas(0, 1)
    deltas(3, 4)
    for_deltas(1, lambda copy: copy.start())

    @pl.when(n < NT - 1)
    def _():
        RX[n, pl.ds(HU, HU)] = TX[n]

    E = 3 * RC_ROWS
    col = iota((W, 128), 1)
    own = (n * SLAB - 16 + col) & (WCO - 1)
    picks = jnp.where(((iota((W, 128), 0) >> 1) == own) & (col < 64), 1.0, 0.0).astype(F32)
    pairs = (iota((RC_ROWS, R), 1) // 2 == iota((RC_ROWS, R), 0)).astype(F32)
    for part, cells in enumerate((WX[0], wet_cells[...], WX[1])):
        window = (jnp.dot(jnp.dot(pairs, cells.astype(F32)), picks) > 3.5).astype(F32)
        for i in range(RC_ROWS):
            WC[part * RC_ROWS + i] = jnp.broadcast_to(window[i:i + 1, :], (L, 128))

    def arrived(s):
        units = (NT - s) // 2
        for phase in range(2):
            for d, there in ((1, up), (-1, down), (0, n != s)):
                if piece(d, phase, units)[1]:
                    @pl.when(there)
                    def _(d=d, phase=phase):
                        delta_arrival(s, d, phase, units).wait_recv()

    def row_of(s, r, f):
        x = RX[s, r // 2 // HU * HU + slot_of(r // 2 % HU), f]
        return x if r % 2 == 0 else rolled(x, 64)

    arrived(0)
    for r in range(E):
        for f in range(3):
            CT[0, r, f] = row_of(0, r, f)

    def result_copy(s):
        return pltpu.make_async_remote_copy(
            src_ref=TC.at[s], dst_ref=RC.at[n], send_sem=tc_send.at[s], recv_sem=rc_recv.at[n],
            device_id=(s, q), device_id_type=MESH)

    def result_arrival(m):
        return pltpu.make_async_remote_copy(
            src_ref=TC.at[0], dst_ref=RC.at[m], send_sem=tc_send.at[0], recv_sem=rc_recv.at[m],
            device_id=(m, q), device_id_type=MESH)

    depth = depth_of(128)
    group = lanes // SLAB
    for s in range(1, NT):
        now, later = CT.at[(s - 1) % 2], CT.at[s % 2]
        h = NT - 1 - s
        lo, hi = RC_ROWS - h, 2 * RC_ROWS + h
        size = (hi - lo + 2) * L
        PC[pl.ds(lo - 1, hi - lo + 2)] = mixed(
            KC[pl.ds(0, size), pl.ds(0, size)], now[pl.ds(lo - 1, hi - lo + 2), 0].reshape(size, 128)
        ).reshape(hi - lo + 2, L, 128)
        if s < NT - 1:
            arrived(s)
        for r in range(lo, hi):
            row = q * RC_ROWS + (r - RC_ROWS)
            f = rotation * (2.0 * (row.astype(F32) + 0.5) / (RC_ROWS * NL) - 1.0)
            inside = (row >= 0) & (row < RC_ROWS * NL)
            new = updated(now, r, PC, depth, WC[r], f, 2.0, None, (0.0, 1.0), STEPS * time_step, inside)
            for i in range(3):
                if RC_ROWS <= r < 2 * RC_ROWS:
                    RES[r - RC_ROWS, i] = new[i]
                if s < NT - 1:
                    later[r, i] = new[i] + row_of(s, r, i)
        for b in range(2):
            for i in range(3):
                packed = rolled(RES[4 * b, i], -16)
                for g in range(1, 4):
                    packed = jnp.where(group == g, rolled(RES[4 * b + g, i], SLAB * g - 16), packed)
                TC[s, b, i] = packed

        @pl.when(n != s)
        def _(s=s):
            result_copy(s).start()

        @pl.when(n == s)
        def _(s=s):
            RC[s] = TC[s]

    @pl.when(n > 0)
    def _():
        @pl.loop(1, NT)
        def _(j):
            result_arrival(lax.rem(n + j, NT)).wait_recv()

        for r in range(RC_ROWS):
            b, g = r // 4, r % 4
            for i in range(3):
                for j in range(WCO // 128):
                    value = rolled(RC[4 * j, b, i], -SLAB * g)
                    for m in range(1, 4):
                        value = jnp.where(group == m, rolled(RC[4 * j + m, b, i], SLAB * (m - g)), value)
                    CN[r, i, :, pl.ds(128 * j, 128)] = value

    change = picked((CN[...] - CO[...]).reshape(-1, WCO), WP[...]).reshape(RC_ROWS, 3, L, W)
    for i in range(3):
        coarse_new[i] = jnp.swapaxes(CN[:, i], 0, 1)
    for r in range(RC_ROWS):
        for i in range(3):
            for more in range(2):
                YA[HALO + 2 * r + more, i] = YA[HALO + 2 * r + more, i] + change[r, i]
    for i in range(3):
        for b in range(R // 8):
            ends[i, :, pl.ds(8 * b, 8), :] = jnp.swapaxes(YA[pl.ds(HALO + 8 * b, 8), i], 0, 1)

    for phase in range(2):
        for_deltas(phase, lambda copy: copy.wait_send())
    for s in range(1, NT):
        @pl.when(n != s)
        def _(s=s):
            result_copy(s).wait_send()


def local(NT, NL, starts, coarse_old, mean_depth, coupling, wet_cells):
    R, W = wet_cells.shape
    L = 8
    C, WCO = R // 2, W // 2
    E = R + 2 * HALO
    vmem = lambda *shape: pltpu.VMEM(shape, F32)
    sems = lambda *shape: pltpu.SemaphoreType.DMA(shape)
    space = pl.BlockSpec(memory_space=pltpu.VMEM)
    far = pl.BlockSpec(memory_space=pltpu.HBM)
    ends, coarse_new = pl.pallas_call(
        functools.partial(kernel, NT, NL),
        out_shape=(jax.ShapeDtypeStruct((3, L, R, W), F32), jax.ShapeDtypeStruct((3, L, C, WCO), F32)),
        in_specs=[far] * 5,
        out_specs=(space, space),
        scratch_shapes=[
            vmem(3, L, R, W), vmem(3, L, C, WCO), vmem(L, L), pltpu.VMEM((R, W), jnp.int32), pltpu.SMEM((L,), F32),
            vmem(L, 128), vmem(L, L, 128), sems(5),
            vmem(E, 3, L, W), vmem(E, 3, L, W), vmem(E, 3, L, W), vmem(3, E, L, W), vmem(E, L, W),
            pltpu.VMEM((2, R, W), jnp.int32), vmem(STEPS, 2, HALO, 3, L, W),
            vmem(3 * C * L, 3 * C * L), vmem(3 * C * L, 3 * C * L),
            vmem(W, W), vmem(WCO, W), vmem(W, WCO), vmem(WCO, W), vmem(C, 3, L, W),
            vmem(NT, C // 2, 3, L, 128), vmem(NT - 1, 3 * C // 2, 3, L, 128),
            vmem(NT, 2, 3, L, 128), vmem(NT, 2, 3, L, 128),
            vmem(2, 3 * C, 3, L, 128), vmem(3 * C, L, 128), vmem(3 * C, L, 128), vmem(C, 3, L, 128),
            vmem(C, 3, L, WCO), vmem(C * 3 * L, W), vmem(C, 3, L, WCO),
            vmem(C + 2, 3, L, WCO), vmem(C + 2, L, WCO), vmem(C, L, WCO),
            sems(STEPS, 2, HALO), sems(STEPS, 2, HALO), sems(2), sems(2), sems(NT, 3, 2), sems(NT - 1, 3, 2), sems(NT), sems(NT),
        ],
        compiler_params=pltpu.CompilerParams(
            collective_id=0, has_side_effects=True, vmem_limit_bytes=63 * 1024 * 1024),
    )(starts[0], coarse_old[0], mean_depth, coupling, wet_cells)
    return ends[None], coarse_new[None]


def solution(mesh):
    NT, NL = mesh.shape["tm"], mesh.shape["lat"]
    in_specs = (
        P("tm", None, None, "lat", None),
        P("tm", None, None, "lat", None),
        P(),
        P(),
        P("lat", None),
    )
    out_specs = (P("tm", None, None, "lat", None), P("tm", None, None, "lat", None))
    return jax.shard_map(functools.partial(local, NT, NL), mesh=mesh, in_specs=in_specs, out_specs=out_specs,
                         check_vma=False)
```

```python
import functools

import jax
import jax.numpy as jnp
from jax import lax
from jax.experimental import pallas as pl
from jax.experimental.pallas import tpu as pltpu
from jax.sharding import PartitionSpec as P

MESH = pl.DeviceIdType.MESH
F32 = jnp.float32

STEPS = 4
time_step = 0.15
viscosity = 0.02
rotation = 0.3

HALO = 3


def iota(shape, dim):
    return lax.broadcasted_iota(jnp.int32, shape, dim)


def dot(a, b):
    return jnp.dot(a, b, precision=lax.Precision.HIGHEST, preferred_element_type=F32)


def split(x, terms):
    parts = []
    for _ in range(terms):
        part = x.astype(jnp.bfloat16)
        parts.append(part)
        x = x - part.astype(F32)
    return parts


def picked(x, selector):
    rows = x.shape[0]
    result = jnp.dot(jnp.concatenate(split(x, 3), axis=0), selector, preferred_element_type=F32)
    return result[:rows] + (result[rows:2 * rows] + result[2 * rows:])


def mixed(matrix, x):
    high, low = split(matrix, 2)
    x_high, x_low = split(x, 2)
    product = lambda a, b: jnp.dot(a, b, preferred_element_type=F32)
    return product(high, x_high) + (product(high, x_low) + product(low, x_high))


def widened(x, width):
    return x if width == x.shape[1] else jnp.concatenate([x] * (width // x.shape[1]), axis=1)


def rolled(x, shift):
    return pltpu.roll(x, shift % x.shape[-1], axis=x.ndim - 1)


def updated(src, r, p, depth, wet, f, spacing, old, weights, step, inside):
    k = viscosity / (spacing * spacing)
    half = 0.5 / spacing
    e, u, v = src[r, 0], src[r, 1], src[r, 2]
    un, us = src[r + 1, 1], src[r - 1, 1]
    vn, vs = src[r + 1, 2], src[r - 1, 2]
    hvn = (depth + src[r + 1, 0]) * vn
    hvs = (depth + src[r - 1, 0]) * vs
    hu = (depth + e) * u
    pc = p[r]
    ue, uw = rolled(u, -1), rolled(u, 1)
    ve, vw = rolled(v, -1), rolled(v, 1)
    u2, v2 = u * half, v * half
    east, west, north, south = k - u2, k + u2, k - v2, k + v2
    zu = (ue * east + uw * west) + (un * north + us * south)
    zv = (ve * east + vw * west) + (vn * north + vs * south)
    zu = zu + (f * v - (4.0 * k) * u) - (rolled(pc, -1) - rolled(pc, 1))
    zv = zv - (f * u + (4.0 * k) * v) - (p[r + 1] - p[r - 1])
    ze = (rolled(hu, -1) - rolled(hu, 1)) + (hvn - hvs)
    w = wet * step
    ce = jnp.where(inside, -step * half, 0.0).astype(F32)
    out = [ce * ze, w * zu, w * zv]
    first, second = weights
    now = [e, u, v]
    for i in range(3):
        out[i] = out[i] + (now[i] if second == 1.0 else second * now[i])
        if first != 0.0:
            out[i] = out[i] + first * old[r, i]
    return out


def kernel(NT, NL, starts_in, old_in, depth_in, coupling_in, wet_in, ends, coarse_new,
           SV, OV, CV, WV, DS, DP, CF, in_sem, YA, Y1, Y2, PB, WET, WX, HB, KF, KC, WW, W2, WR, DL, TX, RX, TC, RC, CT, PC, WC, RES,
           CO, BW, CN, C0, P0, W0,
           hs_send, hs_recv, wx_send, wx_recv, tx_send, rx_recv, fw_send, fw_recv, tc_send, rc_recv):
    starts, coarse_old, mean_depth, coupling, wet_cells = SV, OV, DS, CV, WV
    R, W = wet_cells.shape
    L = 8
    fetches = [pltpu.make_async_copy(source, target, in_sem.at[i]) for i, (source, target) in enumerate(
        [(starts_in.at[f], SV.at[f]) for f in range(3)] + [(wet_in, WV), (coupling_in, CV), (depth_in, DS), (old_in, OV)])]
    for fetch in fetches:
        fetch.start()
    RC_ROWS, WCO = R // 2, W // 2
    SLAB = WCO // NT
    n, q = lax.axis_index("tm"), lax.axis_index("lat")
    up, down = q > 0, q < NL - 1
    inside_side = {-1: up, 1: down}

    barrier = pltpu.get_barrier_semaphore()

    def greet(m, row):
        pl.semaphore_signal(barrier, inc=1, device_id=(m, row), device_id_type=MESH)

    for j in range(1, NT):
        greet(lax.rem(n + j, NT), q)
    for d in (-1, 1):
        @pl.when(inside_side[d])
        def _(d=d):
            greet(n, q + d)

    for f in range(3):
        fetches[f].wait()
        for b in range(R // 8):
            YA[pl.ds(HALO + 8 * b, 8), f] = jnp.swapaxes(starts[f, :, pl.ds(8 * b, 8), :], 0, 1)

    pl.semaphore_wait(barrier, (NT - 1) + up.astype(jnp.int32) + down.astype(jnp.int32))

    def halo_copy(k, side, j):
        row = HALO + HALO - 1 - j if side == -1 else R + j
        slot = 1 if side == -1 else 0
        return pltpu.make_async_remote_copy(
            src_ref=YA.at[row], dst_ref=HB.at[k, slot, row - HALO if side == -1 else j],
            send_sem=hs_send.at[k, slot, j], recv_sem=hs_recv.at[k, slot, j],
            device_id=(n, q + side), device_id_type=MESH)

    def halo_arrival(k, side, j):
        slot = 0 if side == -1 else 1
        return pltpu.make_async_remote_copy(
            src_ref=YA.at[0], dst_ref=HB.at[k, slot, j if side == -1 else HALO - 1 - j],
            send_sem=hs_send.at[k, slot, j], recv_sem=hs_recv.at[k, slot, j],
            device_id=(n, q + side), device_id_type=MESH)

    def wet_copy(side):
        slot = 1 if side == -1 else 0
        return pltpu.make_async_remote_copy(
            src_ref=wet_cells, dst_ref=WX.at[slot], send_sem=wx_send.at[slot], recv_sem=wx_recv.at[slot],
            device_id=(n, q + side), device_id_type=MESH)

    def send_row(k, j):
        for side in (-1, 1):
            @pl.when(inside_side[side])
            def _(side=side):
                halo_copy(k, side, j).start()

    for j in range(HALO):
        send_row(0, j)
    for fetch in fetches[3:]:
        fetch.wait()
    for side in (-1, 1):
        @pl.when(inside_side[side])
        def _(side=side):
            wet_copy(side).start()

        @pl.when(jnp.logical_not(inside_side[side]))
        def _(side=side):
            slot = 0 if side == -1 else 1
            WX[slot] = jnp.zeros((R, W), jnp.int32)
            YA[pl.ds(0 if side == -1 else HALO + R, HALO)] = jnp.zeros((HALO, 3, L, W), F32)
            RX[:, pl.ds(0 if side == -1 else RC_ROWS, RC_ROWS // 2)] = jnp.zeros(
                (NT - 1, RC_ROWS // 2, 3, L, 128), F32)

    KN = KF.shape[0]
    spread = (iota((KN, L), 0) % L == iota((KN, L), 1)).astype(F32)
    spread_t = (iota((L, KN), 1) % L == iota((L, KN), 0)).astype(F32)
    blocks = dot(dot(spread, coupling[...]), spread_t)
    blocks = jnp.where(iota((KN, KN), 0) // L == iota((KN, KN), 1) // L, blocks, 0.0)
    KF[...] = 0.5 * blocks
    KC[...] = 0.25 * blocks
    for shift in range(L):
        column = (iota((L, L), 0) - shift + L) & (L - 1)
        part = jnp.sum(jnp.where(iota((L, L), 1) == column, coupling[...], 0.0), axis=1, keepdims=True)
        CF[shift] = jnp.broadcast_to(0.5 * part, (L, 128))

    layer = iota((L, 128), 0)
    value = jnp.zeros((L, 128), F32)
    for l in range(L):
        value = jnp.where(layer == l, mean_depth[l], value)
    DP[...] = value

    def depth_of(width):
        return widened(DP[...], width)

    wet_own = wet_cells[...].astype(F32)
    for r in range(R):
        WET[HALO + r] = jnp.broadcast_to(wet_own[r:r + 1, :], (L, W))

    position = iota((8, W), 1)
    target = ((position >> 6) * SLAB - 16 + (position & 63)) & (WCO - 1)
    target = target[:1]
    selector = lambda where: jnp.where(where, 1.0, 0.0).astype(jnp.bfloat16)
    WW[...] = selector((iota((W, W), 0) >> 1) == target)
    W2[...] = selector(iota((WCO, W), 0) == target)
    WR[...] = selector((iota((W, WCO), 0) >> 1) == iota((W, WCO), 1))

    @pl.when(n == 0)
    def _():
        sums = jnp.stack([YA[HALO + 2 * i] + YA[HALO + 1 + 2 * i] for i in range(RC_ROWS)])
        C0[pl.ds(1, RC_ROWS)] = (0.25 * picked(sums.reshape(-1, W), WR[...])).reshape(RC_ROWS, 3, L, WCO)

    for f in range(3):
        CO[:, f] = jnp.swapaxes(coarse_old[f], 0, 1)

    def fine_f(r):
        row = q * R + (r - HALO)
        return rotation * (2.0 * (row.astype(F32) + 0.5) / (R * NL) - 1.0), (row >= 0) & (row < R * NL)

    stages = (
        (YA, Y1, (0.0, 1.0), 1.0),
        (Y1, Y2, (0.75, 0.25), 0.25),
        (Y2, YA, (1.0 / 3.0, 2.0 / 3.0), 2.0 / 3.0),
    )

    def pressure(stage, pieces):
        src = stages[stage][0]
        count = sum(c for _, c in pieces)
        rows = [src[pl.ds(a, c), 0] for a, c in pieces]
        rows = rows[0] if len(rows) == 1 else jnp.concatenate(rows, axis=0)
        size = count * L
        result = mixed(KF[pl.ds(0, size), pl.ds(0, size)], rows.reshape(size, W)).reshape(count, L, W)
        at = 0
        for a, c in pieces:
            PB[stage, pl.ds(a, c)] = result[at:at + c]
            at += c

    def row_pressure(stage, r):
        e = stages[stage][0][r, 0]
        total = widened(CF[0], W) * e
        for shift in range(1, L):
            total = total + widened(CF[shift], W) * pltpu.roll(e, shift, axis=0)
        PB[stage, r] = total

    def fine_row(stage, r):
        src, dst, weights, g = stages[stage]
        f, inside = fine_f(r)
        new = updated(src, r, PB.at[stage], depth_of(W), WET[r], f, 1.0, YA, weights, g * time_step, inside)
        for i in range(3):
            dst[r, i] = new[i]

    def coarse_first():
        sums = jnp.stack([YA[1] + YA[2], YA[HALO + R] + YA[HALO + R + 1]])
        outer = (0.25 * picked(sums.reshape(-1, W), WR[...])).reshape(2, 3, L, WCO)
        C0[0] = outer[0]
        C0[RC_ROWS + 1] = outer[1]
        size = (RC_ROWS + 2) * L
        P0[...] = mixed(KC[pl.ds(0, size), pl.ds(0, size)], C0[:, 0].reshape(size, WCO)).reshape(RC_ROWS + 2, L, WCO)
        pairs = (iota((RC_ROWS, R), 1) // 2 == iota((RC_ROWS, R), 0)).astype(F32)
        wet_full = (jnp.dot(jnp.dot(pairs, wet_cells[...].astype(F32)), WR[...].astype(F32)) > 3.5).astype(F32)
        for i in range(RC_ROWS):
            W0[i] = jnp.broadcast_to(wet_full[i:i + 1, :], (L, WCO))

        @pl.loop(1, RC_ROWS + 1)
        def _(r):
            row = q * RC_ROWS + r - 1
            f = rotation * (2.0 * (row.astype(F32) + 0.5) / (RC_ROWS * NL) - 1.0)
            new = updated(C0, r, P0, depth_of(WCO), W0[r - 1], f, 2.0, None, (0.0, 1.0), STEPS * time_step, True)
            for i in range(3):
                CN[r - 1, i] = new[i]

    HU = RC_ROWS // 2
    lanes = iota((L, 128), 1)

    def slot_of(unit):
        return {1: 0, 2: 1, 0: 2, 3: 3}[unit]

    def deltas(units):
        rows = [2 * unit + more for unit in units for more in range(2)]
        sums = jnp.stack([YA[HALO + 2 * i] + YA[HALO + 1 + 2 * i] for i in rows])
        change = (0.25 * picked(sums.reshape(-1, W), WW[...])).reshape(len(rows), 3, L, W)
        for at, i in enumerate(rows):
            DL[i] = change[at] + BW[pl.ds(i * 3 * L, 3 * L)].reshape(3, L, W)
        for i in units:
            for f in range(3):
                for j in range(NT // 2):
                    a = DL[2 * i, f, :, pl.ds(128 * j, 128)]
                    b = DL[2 * i + 1, f, :, pl.ds(128 * j, 128)]
                    TX[2 * j, slot_of(i), f] = jnp.where(lanes < 64, a, rolled(b, 64))
                    TX[2 * j + 1, slot_of(i), f] = jnp.where(lanes < 64, rolled(a, 64), b)

    def piece(d, phase, units):
        if d == 0 or units == 4:
            return 2 * phase, 2
        if phase == 1:
            return (3 if d == 1 else 2), 1
        return {1: (0, 0), 2: (1 if d == 1 else 0, 1), 3: (0, 2)}[units]

    def delta_copy(m, phase):
        return pltpu.make_async_remote_copy(
            src_ref=TX.at[m, pl.ds(2 * phase, 2)], dst_ref=RX.at[n, pl.ds(HU + 2 * phase, 2)],
            send_sem=tx_send.at[m, phase], recv_sem=rx_recv.at[n, phase],
            device_id=(m, q), device_id_type=MESH)

    def delta_arrival(s, phase):
        return pltpu.make_async_remote_copy(
            src_ref=TX.at[0, pl.ds(0, 2)], dst_ref=RX.at[s, pl.ds(HU + 2 * phase, 2)],
            send_sem=tx_send.at[0, phase], recv_sem=rx_recv.at[s, phase],
            device_id=(s, q), device_id_type=MESH)

    def for_deltas(phase, act):
        @pl.when(n < NT - 1)
        def _():
            @pl.loop(1, NT)
            def _(j):
                act(delta_copy(lax.rem(n + j, NT), phase))

    def send_deltas(phase):
        for_deltas(phase, lambda copy: copy.start())

        @pl.when(n < NT - 1)
        def _():
            RX[n, pl.ds(HU + 2 * phase, 2)] = TX[n, pl.ds(2 * phase, 2)]

    def passing(s, d, phase):
        first, count = piece(d, phase, (NT - s) // 2)
        side = 0 if d == 1 else 1
        return pltpu.make_async_remote_copy(
            src_ref=RX.at[s, pl.ds(HU + first, count)], dst_ref=RX.at[s, pl.ds(HU * (1 - d) + first, count)],
            send_sem=fw_send.at[s, side, phase], recv_sem=fw_recv.at[s, side, phase],
            device_id=(n, q + d), device_id_type=MESH)

    def passed_on(phase):
        return [(s, d, there) for s in range(NT - 1) for d, there in ((1, down), (-1, up))
                if piece(d, phase, (NT - s) // 2)[1]]

    def pass_deltas(phase):
        for s in range(NT - 1):
            @pl.when(n != s)
            def _(s=s):
                delta_arrival(s, phase).wait_recv()
            for t, d, there in passed_on(phase):
                if t == s:
                    @pl.when(there)
                    def _(s=s, d=d):
                        passing(s, d, phase).start()

    @pl.loop(0, STEPS)
    def _(k):
        for stage in range(3):
            pressure(stage, [(HALO + stage, R - 2 * stage)])

            for r in range(R - 2 * (stage + 1)):
                fine_row(stage, HALO + stage + 1 + r)

        @pl.when(k == STEPS - 1)
        def _():
            deltas((1, 2))
            send_deltas(0)

        for side in (-1, 1):
            slot = 0 if side == -1 else 1

            @pl.when(inside_side[side])
            def _(side=side, slot=slot):
                for j in range(HALO):
                    halo_arrival(k, side, j).wait_recv()
                YA[pl.ds(0 if side == -1 else HALO + R, HALO)] = HB[k, slot]
                for j in range(HALO):
                    halo_copy(k, side, j).wait_send()

        @pl.when(k == 0)
        def _():
            for side in (-1, 1):
                @pl.when(inside_side[side])
                def _(side=side):
                    wet_copy(side).wait_send()
                    wet_copy(-side).wait_recv()
            for r in range(HALO):
                WET[r] = jnp.broadcast_to(WX[0, R - HALO + r:R - HALO + r + 1, :].astype(F32), (L, W))
                WET[HALO + R + r] = jnp.broadcast_to(WX[1, r:r + 1, :].astype(F32), (L, W))

        for j in range(HALO):
            for stage in range(3):
                low, high = HALO - j + stage, HALO + R - 1 + j - stage
                row_pressure(stage, low - 1)
                row_pressure(stage, high + 1)
                fine_row(stage, low)
                fine_row(stage, high)

            @pl.when(k < STEPS - 1)
            def _(j=j):
                send_row(k + 1, j)

        @pl.when(k == 0)
        def _():
            @pl.when(n == 0)
            def _():
                coarse_first()
                BW[...] = picked((CN[...] - CO[...]).reshape(-1, WCO), W2[...])

            @pl.when(n > 0)
            def _():
                BW[...] = picked((-CO[...]).reshape(-1, WCO), W2[...])

    keep = pltpu.make_async_copy(YA.at[pl.ds(HALO, R)], ends, in_sem.at[5 + 2])
    keep.start()
    deltas((0, 3))
    send_deltas(1)
    pass_deltas(0)

    E = 3 * RC_ROWS
    col = iota((W, 128), 1)
    own = (n * SLAB - 16 + col) & (WCO - 1)
    picks = jnp.where(((iota((W, 128), 0) >> 1) == own) & (col < 64), 1.0, 0.0).astype(F32)
    pairs = (iota((RC_ROWS, R), 1) // 2 == iota((RC_ROWS, R), 0)).astype(F32)
    for part, cells in enumerate((WX[0], wet_cells[...], WX[1])):
        window = (jnp.dot(jnp.dot(pairs, cells.astype(F32)), picks) > 3.5).astype(F32)
        for i in range(RC_ROWS):
            WC[part * RC_ROWS + i] = jnp.broadcast_to(window[i:i + 1, :], (L, 128))

    pass_deltas(1)

    def arrived(s):
        for phase in range(2):
            for t, d, _ in passed_on(phase):
                if t == s:
                    @pl.when(up if d == 1 else down)
                    def _(d=d, phase=phase):
                        passing(s, d, phase).wait_recv()

    def row_of(s, r, f):
        x = RX[s, r // 2 // HU * HU + slot_of(r // 2 % HU), f]
        return x if r % 2 == 0 else rolled(x, 64)

    arrived(0)
    for r in range(E):
        for f in range(3):
            CT[0, r, f] = row_of(0, r, f)

    def result_copy(s):
        return pltpu.make_async_remote_copy(
            src_ref=TC.at[s], dst_ref=RC.at[n], send_sem=tc_send.at[s], recv_sem=rc_recv.at[n],
            device_id=(s, q), device_id_type=MESH)

    def result_arrival(m):
        return pltpu.make_async_remote_copy(
            src_ref=TC.at[0], dst_ref=RC.at[m], send_sem=tc_send.at[0], recv_sem=rc_recv.at[m],
            device_id=(m, q), device_id_type=MESH)

    depth = depth_of(128)
    group = lanes // SLAB
    for s in range(1, NT):
        now, later = CT.at[(s - 1) % 2], CT.at[s % 2]
        h = NT - 1 - s
        lo, hi = RC_ROWS - h, 2 * RC_ROWS + h
        for r in range(lo - 1, hi + 1):
            e = now[r, 0]
            total = (0.5 * CF[0]) * e
            for shift in range(1, L):
                total = total + (0.5 * CF[shift]) * pltpu.roll(e, shift, axis=0)
            PC[r] = total
        if s < NT - 1:
            arrived(s)
        for r in range(lo, hi):
            row = q * RC_ROWS + (r - RC_ROWS)
            f = rotation * (2.0 * (row.astype(F32) + 0.5) / (RC_ROWS * NL) - 1.0)
            inside = (row >= 0) & (row < RC_ROWS * NL)
            new = updated(now, r, PC, depth, WC[r], f, 2.0, None, (0.0, 1.0), STEPS * time_step, inside)
            for i in range(3):
                if RC_ROWS <= r < 2 * RC_ROWS:
                    RES[r - RC_ROWS, i] = new[i]
                if s < NT - 1:
                    later[r, i] = new[i] + row_of(s, r, i)
        for b in range(2):
            for i in range(3):
                packed = rolled(RES[4 * b, i], -16)
                for g in range(1, 4):
                    packed = jnp.where(group == g, rolled(RES[4 * b + g, i], SLAB * g - 16), packed)
                TC[s, b, i] = packed

        @pl.when(n != s)
        def _(s=s):
            result_copy(s).start()

        @pl.when(n == s)
        def _(s=s):
            RC[s] = TC[s]

    @pl.when(n > 0)
    def _():
        @pl.loop(1, NT)
        def _(j):
            result_arrival(lax.rem(n + j, NT)).wait_recv()

        for r in range(RC_ROWS):
            b, g = r // 4, r % 4
            for i in range(3):
                for j in range(WCO // 128):
                    value = rolled(RC[4 * j, b, i], -SLAB * g)
                    for m in range(1, 4):
                        value = jnp.where(group == m, rolled(RC[4 * j + m, b, i], SLAB * (m - g)), value)
                    CN[r, i, :, pl.ds(128 * j, 128)] = value

    coarse_new[...] = CN[...]
    keep.wait()
    for phase in range(2):
        for_deltas(phase, lambda copy: copy.wait_send())
        for s, d, there in passed_on(phase):
            @pl.when(there)
            def _(s=s, d=d, phase=phase):
                passing(s, d, phase).wait_send()
    for s in range(1, NT):
        @pl.when(n != s)
        def _(s=s):
            result_copy(s).wait_send()


def correct(state, coarse_new, coarse_old, ends, result, WP):
    R, _, L, W = state.shape
    C, WCO = R // 2, W // 2

    @pl.when(pl.program_id(0) == 0)
    def _():
        WP[...] = jnp.where((iota((WCO, W), 1) >> 1) == iota((WCO, W), 0), 1.0, 0.0).astype(jnp.bfloat16)

    new = coarse_new[:, 0]
    result[0] = jnp.swapaxes(new, 0, 1)
    change = new - jnp.swapaxes(coarse_old[0], 0, 1)
    change = picked(change.reshape(C * L, WCO), WP[...]).reshape(C, L, W)
    for b in range(R // 8):
        rows = jnp.stack([state[8 * b + i, 0] + change[4 * b + i // 2] for i in range(8)])
        ends[0, :, pl.ds(8 * b, 8), :] = jnp.swapaxes(rows, 0, 1)


def local(NT, NL, starts, coarse_old, mean_depth, coupling, wet_cells):
    R, W = wet_cells.shape
    L = 8
    C, WCO = R // 2, W // 2
    E = R + 2 * HALO
    vmem = lambda *shape: pltpu.VMEM(shape, F32)
    half = lambda *shape: pltpu.VMEM(shape, jnp.bfloat16)
    sems = lambda *shape: pltpu.SemaphoreType.DMA(shape)
    space = pl.BlockSpec(memory_space=pltpu.VMEM)
    far = pl.BlockSpec(memory_space=pltpu.HBM)
    state, coarse_new = pl.pallas_call(
        functools.partial(kernel, NT, NL),
        out_shape=(jax.ShapeDtypeStruct((R, 3, L, W), F32), jax.ShapeDtypeStruct((C, 3, L, WCO), F32)),
        in_specs=[far] * 5,
        out_specs=(far, space),
        scratch_shapes=[
            vmem(3, L, R, W), vmem(3, L, C, WCO), vmem(L, L), pltpu.VMEM((R, W), jnp.int32), pltpu.SMEM((L,), F32),
            vmem(L, 128), vmem(L, L, 128), sems(8),
            vmem(E, 3, L, W), vmem(E, 3, L, W), vmem(E, 3, L, W), vmem(3, E, L, W), vmem(E, L, W),
            pltpu.VMEM((2, R, W), jnp.int32), vmem(STEPS, 2, HALO, 3, L, W),
            vmem(3 * C * L, 3 * C * L), vmem(3 * C * L, 3 * C * L),
            half(W, W), half(WCO, W), half(W, WCO), vmem(C, 3, L, W),
            vmem(NT, C // 2, 3, L, 128), vmem(NT - 1, 3 * C // 2, 3, L, 128),
            vmem(NT, 2, 3, L, 128), vmem(NT, 2, 3, L, 128),
            vmem(2, 3 * C, 3, L, 128), vmem(3 * C, L, 128), vmem(3 * C, L, 128), vmem(C, 3, L, 128),
            vmem(C, 3, L, WCO), vmem(C * 3 * L, W), vmem(C, 3, L, WCO),
            vmem(C + 2, 3, L, WCO), vmem(C + 2, L, WCO), vmem(C, L, WCO),
            sems(STEPS, 2, HALO), sems(STEPS, 2, HALO), sems(2), sems(2), sems(NT, 2), sems(NT - 1, 2), sems(NT - 1, 2, 2), sems(NT - 1, 2, 2), sems(NT), sems(NT),
        ],
        compiler_params=pltpu.CompilerParams(
            collective_id=0, has_side_effects=True, vmem_limit_bytes=63 * 1024 * 1024),
    )(starts[0], coarse_old[0], mean_depth, coupling, wet_cells)
    ends, result = pl.pallas_call(
        correct,
        grid=(3,),
        out_shape=(jax.ShapeDtypeStruct((3, L, R, W), F32), jax.ShapeDtypeStruct((3, L, C, WCO), F32)),
        in_specs=[
            pl.BlockSpec((R, 1, L, W), lambda f: (0, f, 0, 0)),
            pl.BlockSpec((C, 1, L, WCO), lambda f: (0, f, 0, 0)),
            pl.BlockSpec((1, L, C, WCO), lambda f: (f, 0, 0, 0)),
        ],
        out_specs=(pl.BlockSpec((1, L, R, W), lambda f: (f, 0, 0, 0)), pl.BlockSpec((1, L, C, WCO), lambda f: (f, 0, 0, 0))),
        scratch_shapes=[pltpu.VMEM((WCO, W), jnp.bfloat16)],
        compiler_params=pltpu.CompilerParams(vmem_limit_bytes=63 * 1024 * 1024),
    )(state, coarse_new, coarse_old[0])
    return ends[None], result[None]


def solution(mesh):
    NT, NL = mesh.shape["tm"], mesh.shape["lat"]
    in_specs = (
        P("tm", None, None, "lat", None),
        P("tm", None, None, "lat", None),
        P(),
        P(),
        P("lat", None),
    )
    out_specs = (P("tm", None, None, "lat", None), P("tm", None, None, "lat", None))
    return jax.shard_map(functools.partial(local, NT, NL), mesh=mesh, in_specs=in_specs, out_specs=out_specs,
                         check_vma=False)
```

```python
import functools

import jax
import jax.numpy as jnp
from jax import lax
from jax.experimental import pallas as pl
from jax.experimental.pallas import tpu as pltpu
from jax.sharding import PartitionSpec as P

MESH = pl.DeviceIdType.MESH
F32 = jnp.float32

STEPS = 4
time_step = 0.15
viscosity = 0.02
rotation = 0.3

HALO = 3


def iota(shape, dim):
    return lax.broadcasted_iota(jnp.int32, shape, dim)


def dot(a, b):
    return jnp.dot(a, b, precision=lax.Precision.HIGHEST, preferred_element_type=F32)


def split(x, terms):
    parts = []
    for _ in range(terms):
        part = x.astype(jnp.bfloat16)
        parts.append(part)
        x = x - part.astype(F32)
    return parts


def picked(x, selector):
    rows = x.shape[0]
    result = jnp.dot(jnp.concatenate(split(x, 3), axis=0), selector, preferred_element_type=F32)
    return result[:rows] + (result[rows:2 * rows] + result[2 * rows:])


def mixed(matrix, x):
    high, low = split(matrix, 2)
    x_high, x_low = split(x, 2)
    product = lambda a, b: jnp.dot(a, b, preferred_element_type=F32)
    return product(high, x_high) + (product(high, x_low) + product(low, x_high))


def widened(x, width):
    return x if width == x.shape[1] else jnp.concatenate([x] * (width // x.shape[1]), axis=1)


def rolled(x, shift):
    return pltpu.roll(x, shift % x.shape[-1], axis=x.ndim - 1)


def updated(src, r, p, depth, wet, f, spacing, old, weights, step, inside):
    k = viscosity / (spacing * spacing)
    half = 0.5 / spacing
    e, u, v = src[r, 0], src[r, 1], src[r, 2]
    un, us = src[r + 1, 1], src[r - 1, 1]
    vn, vs = src[r + 1, 2], src[r - 1, 2]
    hvn = (depth + src[r + 1, 0]) * vn
    hvs = (depth + src[r - 1, 0]) * vs
    hu = (depth + e) * u
    pc = p[r]
    ue, uw = rolled(u, -1), rolled(u, 1)
    ve, vw = rolled(v, -1), rolled(v, 1)
    u2, v2 = u * half, v * half
    east, west, north, south = k - u2, k + u2, k - v2, k + v2
    zu = (ue * east + uw * west) + (un * north + us * south)
    zv = (ve * east + vw * west) + (vn * north + vs * south)
    zu = zu + (f * v - (4.0 * k) * u) - (rolled(pc, -1) - rolled(pc, 1))
    zv = zv - (f * u + (4.0 * k) * v) - (p[r + 1] - p[r - 1])
    ze = (rolled(hu, -1) - rolled(hu, 1)) + (hvn - hvs)
    w = wet * step
    ce = jnp.where(inside, -step * half, 0.0).astype(F32)
    out = [ce * ze, w * zu, w * zv]
    first, second = weights
    now = [e, u, v]
    for i in range(3):
        out[i] = out[i] + (now[i] if second == 1.0 else second * now[i])
        if first != 0.0:
            out[i] = out[i] + first * old[r, i]
    return out


def kernel(NT, NL, starts_in, old_in, depth_in, coupling_in, wet_in, ends, coarse_new,
           SV, OV, CV, WV, DS, DP, CF, in_sem, YA, Y1, Y2, PB, WET, WX, HB, KF, KC, WW, W2, WR, DL, TX, RX, TC, RC, CT, PC, WC, RES,
           CO, BW, CN, C0, P0, W0,
           hs_send, hs_recv, wx_send, wx_recv, tx_send, rx_recv, fw_send, fw_recv, tc_send, rc_recv):
    starts, coarse_old, mean_depth, coupling, wet_cells = SV, OV, DS, CV, WV
    R, W = wet_cells.shape
    L = 8
    fetches = [pltpu.make_async_copy(source, target, in_sem.at[i]) for i, (source, target) in enumerate(
        [(starts_in.at[f], SV.at[f]) for f in range(3)] + [(wet_in, WV), (coupling_in, CV), (depth_in, DS), (old_in, OV)])]
    for fetch in fetches:
        fetch.start()
    RC_ROWS, WCO = R // 2, W // 2
    SLAB = WCO // NT
    n, q = lax.axis_index("tm"), lax.axis_index("lat")
    up, down = q > 0, q < NL - 1
    inside_side = {-1: up, 1: down}

    barrier = pltpu.get_barrier_semaphore()

    def greet(m, row):
        pl.semaphore_signal(barrier, inc=1, device_id=(m, row), device_id_type=MESH)

    for j in range(1, NT):
        greet(lax.rem(n + j, NT), q)
    for d in (-1, 1):
        @pl.when(inside_side[d])
        def _(d=d):
            greet(n, q + d)

    pl.semaphore_wait(barrier, (NT - 1) + up.astype(jnp.int32) + down.astype(jnp.int32))
    for f in range(3):
        fetches[f].wait()
        for b in range(R // 8):
            YA[pl.ds(HALO + 8 * b, 8), f] = jnp.swapaxes(starts[f, :, pl.ds(8 * b, 8), :], 0, 1)
        for side in (-1, 1):
            @pl.when(inside_side[side])
            def _(f=f, side=side):
                slot = 1 if side == -1 else 0
                pltpu.make_async_remote_copy(
                    src_ref=YA.at[pl.ds(HALO if side == -1 else R, HALO), f], dst_ref=HB.at[0, slot, :, f],
                    send_sem=hs_send.at[0, slot, f], recv_sem=hs_recv.at[0, slot, f],
                    device_id=(n, q + side), device_id_type=MESH).start()


    def halo_copy(k, side, j):
        row = HALO + HALO - 1 - j if side == -1 else R + j
        slot = 1 if side == -1 else 0
        return pltpu.make_async_remote_copy(
            src_ref=YA.at[row], dst_ref=HB.at[k, slot, row - HALO if side == -1 else j],
            send_sem=hs_send.at[k, slot, j], recv_sem=hs_recv.at[k, slot, j],
            device_id=(n, q + side), device_id_type=MESH)

    def halo_arrival(k, side, j):
        slot = 0 if side == -1 else 1
        return pltpu.make_async_remote_copy(
            src_ref=YA.at[0], dst_ref=HB.at[k, slot, j if side == -1 else HALO - 1 - j],
            send_sem=hs_send.at[k, slot, j], recv_sem=hs_recv.at[k, slot, j],
            device_id=(n, q + side), device_id_type=MESH)

    def wet_copy(side):
        slot = 1 if side == -1 else 0
        return pltpu.make_async_remote_copy(
            src_ref=wet_cells, dst_ref=WX.at[slot], send_sem=wx_send.at[slot], recv_sem=wx_recv.at[slot],
            device_id=(n, q + side), device_id_type=MESH)

    def send_row(k, j):
        for side in (-1, 1):
            @pl.when(inside_side[side])
            def _(side=side):
                halo_copy(k, side, j).start()

    for fetch in fetches[3:]:
        fetch.wait()
    for side in (-1, 1):
        @pl.when(inside_side[side])
        def _(side=side):
            wet_copy(side).start()

        @pl.when(jnp.logical_not(inside_side[side]))
        def _(side=side):
            slot = 0 if side == -1 else 1
            WX[slot] = jnp.zeros((R, W), jnp.int32)
            YA[pl.ds(0 if side == -1 else HALO + R, HALO)] = jnp.zeros((HALO, 3, L, W), F32)
            RX[:, pl.ds(0 if side == -1 else RC_ROWS, RC_ROWS // 2)] = jnp.zeros(
                (NT - 1, RC_ROWS // 2, 3, L, 128), F32)

    KN = KF.shape[0]
    spread = (iota((KN, L), 0) % L == iota((KN, L), 1)).astype(F32)
    spread_t = (iota((L, KN), 1) % L == iota((L, KN), 0)).astype(F32)
    blocks = dot(dot(spread, coupling[...]), spread_t)
    blocks = jnp.where(iota((KN, KN), 0) // L == iota((KN, KN), 1) // L, blocks, 0.0)
    KF[...] = 0.5 * blocks
    KC[...] = 0.25 * blocks
    for shift in range(L):
        column = (iota((L, L), 0) - shift + L) & (L - 1)
        part = jnp.sum(jnp.where(iota((L, L), 1) == column, coupling[...], 0.0), axis=1, keepdims=True)
        CF[shift] = jnp.broadcast_to(0.5 * part, (L, 128))

    layer = iota((L, 128), 0)
    value = jnp.zeros((L, 128), F32)
    for l in range(L):
        value = jnp.where(layer == l, mean_depth[l], value)
    DP[...] = value

    def depth_of(width):
        return widened(DP[...], width)

    wet_own = wet_cells[...].astype(F32)
    for r in range(R):
        WET[HALO + r] = jnp.broadcast_to(wet_own[r:r + 1, :], (L, W))

    position = iota((8, W), 1)
    target = ((position >> 6) * SLAB - 16 + (position & 63)) & (WCO - 1)
    target = target[:1]
    selector = lambda where: jnp.where(where, 1.0, 0.0).astype(jnp.bfloat16)
    WW[...] = selector((iota((W, W), 0) >> 1) == target)
    W2[...] = selector(iota((WCO, W), 0) == target)
    WR[...] = selector((iota((W, WCO), 0) >> 1) == iota((W, WCO), 1))

    @pl.when(n == 0)
    def _():
        sums = jnp.stack([YA[HALO + 2 * i] + YA[HALO + 1 + 2 * i] for i in range(RC_ROWS)])
        C0[pl.ds(1, RC_ROWS)] = (0.25 * picked(sums.reshape(-1, W), WR[...])).reshape(RC_ROWS, 3, L, WCO)

    for f in range(3):
        CO[:, f] = jnp.swapaxes(coarse_old[f], 0, 1)

    def fine_f(r):
        row = q * R + (r - HALO)
        return rotation * (2.0 * (row.astype(F32) + 0.5) / (R * NL) - 1.0), (row >= 0) & (row < R * NL)

    stages = (
        (YA, Y1, (0.0, 1.0), 1.0),
        (Y1, Y2, (0.75, 0.25), 0.25),
        (Y2, YA, (1.0 / 3.0, 2.0 / 3.0), 2.0 / 3.0),
    )

    def pressure(stage, pieces):
        src = stages[stage][0]
        count = sum(c for _, c in pieces)
        rows = [src[pl.ds(a, c), 0] for a, c in pieces]
        rows = rows[0] if len(rows) == 1 else jnp.concatenate(rows, axis=0)
        size = count * L
        result = mixed(KF[pl.ds(0, size), pl.ds(0, size)], rows.reshape(size, W)).reshape(count, L, W)
        at = 0
        for a, c in pieces:
            PB[stage, pl.ds(a, c)] = result[at:at + c]
            at += c

    def row_pressure(stage, r):
        e = stages[stage][0][r, 0]
        total = widened(CF[0], W) * e
        for shift in range(1, L):
            total = total + widened(CF[shift], W) * pltpu.roll(e, shift, axis=0)
        PB[stage, r] = total

    def fine_row(stage, r):
        src, dst, weights, g = stages[stage]
        f, inside = fine_f(r)
        new = updated(src, r, PB.at[stage], depth_of(W), WET[r], f, 1.0, YA, weights, g * time_step, inside)
        for i in range(3):
            dst[r, i] = new[i]

    def coarse_first():
        sums = jnp.stack([YA[1] + YA[2], YA[HALO + R] + YA[HALO + R + 1]])
        outer = (0.25 * picked(sums.reshape(-1, W), WR[...])).reshape(2, 3, L, WCO)
        C0[0] = outer[0]
        C0[RC_ROWS + 1] = outer[1]
        size = (RC_ROWS + 2) * L
        P0[...] = mixed(KC[pl.ds(0, size), pl.ds(0, size)], C0[:, 0].reshape(size, WCO)).reshape(RC_ROWS + 2, L, WCO)
        pairs = (iota((RC_ROWS, R), 1) // 2 == iota((RC_ROWS, R), 0)).astype(F32)
        wet_full = (jnp.dot(jnp.dot(pairs, wet_cells[...].astype(F32)), WR[...].astype(F32)) > 3.5).astype(F32)
        for i in range(RC_ROWS):
            W0[i] = jnp.broadcast_to(wet_full[i:i + 1, :], (L, WCO))

        @pl.loop(1, RC_ROWS + 1)
        def _(r):
            row = q * RC_ROWS + r - 1
            f = rotation * (2.0 * (row.astype(F32) + 0.5) / (RC_ROWS * NL) - 1.0)
            new = updated(C0, r, P0, depth_of(WCO), W0[r - 1], f, 2.0, None, (0.0, 1.0), STEPS * time_step, True)
            for i in range(3):
                CN[r - 1, i] = new[i]

    HU = RC_ROWS // 2
    lanes = iota((L, 128), 1)

    def slot_of(unit):
        return {1: 0, 2: 1, 0: 2, 3: 3}[unit]

    def deltas(units):
        rows = [2 * unit + more for unit in units for more in range(2)]
        sums = jnp.stack([YA[HALO + 2 * i] + YA[HALO + 1 + 2 * i] for i in rows])
        change = (0.25 * picked(sums.reshape(-1, W), WW[...])).reshape(len(rows), 3, L, W)
        for at, i in enumerate(rows):
            DL[i] = change[at] + BW[pl.ds(i * 3 * L, 3 * L)].reshape(3, L, W)
        for i in units:
            for f in range(3):
                for j in range(NT // 2):
                    a = DL[2 * i, f, :, pl.ds(128 * j, 128)]
                    b = DL[2 * i + 1, f, :, pl.ds(128 * j, 128)]
                    TX[2 * j, slot_of(i), f] = jnp.where(lanes < 64, a, rolled(b, 64))
                    TX[2 * j + 1, slot_of(i), f] = jnp.where(lanes < 64, rolled(a, 64), b)

    def piece(d, phase, units):
        if d == 0 or units == 4:
            return 2 * phase, 2
        if phase == 1:
            return (3 if d == 1 else 2), 1
        return {1: (0, 0), 2: (1 if d == 1 else 0, 1), 3: (0, 2)}[units]

    def delta_copy(m, phase):
        return pltpu.make_async_remote_copy(
            src_ref=TX.at[m, pl.ds(2 * phase, 2)], dst_ref=RX.at[n, pl.ds(HU + 2 * phase, 2)],
            send_sem=tx_send.at[m, phase], recv_sem=rx_recv.at[n, phase],
            device_id=(m, q), device_id_type=MESH)

    def delta_arrival(s, phase):
        return pltpu.make_async_remote_copy(
            src_ref=TX.at[0, pl.ds(0, 2)], dst_ref=RX.at[s, pl.ds(HU + 2 * phase, 2)],
            send_sem=tx_send.at[0, phase], recv_sem=rx_recv.at[s, phase],
            device_id=(s, q), device_id_type=MESH)

    def for_deltas(phase, act):
        @pl.when(n < NT - 1)
        def _():
            @pl.loop(1, NT)
            def _(j):
                act(delta_copy(lax.rem(n + j, NT), phase))

    def send_deltas(phase):
        for_deltas(phase, lambda copy: copy.start())

        @pl.when(n < NT - 1)
        def _():
            RX[n, pl.ds(HU + 2 * phase, 2)] = TX[n, pl.ds(2 * phase, 2)]

    def passing(s, d, phase):
        first, count = piece(d, phase, (NT - s) // 2)
        side = 0 if d == 1 else 1
        return pltpu.make_async_remote_copy(
            src_ref=RX.at[s, pl.ds(HU + first, count)], dst_ref=RX.at[s, pl.ds(HU * (1 - d) + first, count)],
            send_sem=fw_send.at[s, side, phase], recv_sem=fw_recv.at[s, side, phase],
            device_id=(n, q + d), device_id_type=MESH)

    def passed_on(phase):
        return [(s, d, there) for s in range(NT - 1) for d, there in ((1, down), (-1, up))
                if piece(d, phase, (NT - s) // 2)[1]]

    def pass_deltas(phase):
        for s in range(NT - 1):
            @pl.when(n != s)
            def _(s=s):
                delta_arrival(s, phase).wait_recv()
            for t, d, there in passed_on(phase):
                if t == s:
                    @pl.when(there)
                    def _(s=s, d=d):
                        passing(s, d, phase).start()

    @pl.loop(0, STEPS)
    def _(k):
        for stage in range(3):
            pressure(stage, [(HALO + stage, R - 2 * stage)])

            for r in range(R - 2 * (stage + 1)):
                fine_row(stage, HALO + stage + 1 + r)

        @pl.when(k == STEPS - 1)
        def _():
            deltas((1, 2))
            send_deltas(0)

        for side in (-1, 1):
            slot = 0 if side == -1 else 1

            @pl.when(inside_side[side])
            def _(side=side, slot=slot):
                for j in range(HALO):
                    halo_arrival(k, side, j).wait_recv()
                YA[pl.ds(0 if side == -1 else HALO + R, HALO)] = HB[k, slot]
                for j in range(HALO):
                    halo_copy(k, side, j).wait_send()

        @pl.when(k == 0)
        def _():
            for side in (-1, 1):
                @pl.when(inside_side[side])
                def _(side=side):
                    wet_copy(side).wait_send()
                    wet_copy(-side).wait_recv()
            for r in range(HALO):
                WET[r] = jnp.broadcast_to(WX[0, R - HALO + r:R - HALO + r + 1, :].astype(F32), (L, W))
                WET[HALO + R + r] = jnp.broadcast_to(WX[1, r:r + 1, :].astype(F32), (L, W))

        for j in range(HALO):
            for stage in range(3):
                low, high = HALO - j + stage, HALO + R - 1 + j - stage
                row_pressure(stage, low - 1)
                row_pressure(stage, high + 1)
                fine_row(stage, low)
                fine_row(stage, high)

            @pl.when(k < STEPS - 1)
            def _(j=j):
                send_row(k + 1, j)

        @pl.when(k == 0)
        def _():
            @pl.when(n == 0)
            def _():
                coarse_first()
                BW[...] = picked((CN[...] - CO[...]).reshape(-1, WCO), W2[...])

            @pl.when(n > 0)
            def _():
                BW[...] = picked((-CO[...]).reshape(-1, WCO), W2[...])

    keep = pltpu.make_async_copy(YA.at[pl.ds(HALO, R)], ends, in_sem.at[5 + 2])
    keep.start()
    deltas((0, 3))
    send_deltas(1)
    pass_deltas(0)

    E = 3 * RC_ROWS
    col = iota((W, 128), 1)
    own = (n * SLAB - 16 + col) & (WCO - 1)
    picks = jnp.where(((iota((W, 128), 0) >> 1) == own) & (col < 64), 1.0, 0.0).astype(F32)
    pairs = (iota((RC_ROWS, R), 1) // 2 == iota((RC_ROWS, R), 0)).astype(F32)
    for part, cells in enumerate((WX[0], wet_cells[...], WX[1])):
        window = (jnp.dot(jnp.dot(pairs, cells.astype(F32)), picks) > 3.5).astype(F32)
        for i in range(RC_ROWS):
            WC[part * RC_ROWS + i] = jnp.broadcast_to(window[i:i + 1, :], (L, 128))

    pass_deltas(1)

    def arrived(s):
        for phase in range(2):
            for t, d, _ in passed_on(phase):
                if t == s:
                    @pl.when(up if d == 1 else down)
                    def _(d=d, phase=phase):
                        passing(s, d, phase).wait_recv()

    def row_of(s, r, f):
        x = RX[s, r // 2 // HU * HU + slot_of(r // 2 % HU), f]
        return x if r % 2 == 0 else rolled(x, 64)

    arrived(0)
    for r in range(E):
        for f in range(3):
            CT[0, r, f] = row_of(0, r, f)

    def result_copy(s):
        return pltpu.make_async_remote_copy(
            src_ref=TC.at[s], dst_ref=RC.at[n], send_sem=tc_send.at[s], recv_sem=rc_recv.at[n],
            device_id=(s, q), device_id_type=MESH)

    def result_arrival(m):
        return pltpu.make_async_remote_copy(
            src_ref=TC.at[0], dst_ref=RC.at[m], send_sem=tc_send.at[0], recv_sem=rc_recv.at[m],
            device_id=(m, q), device_id_type=MESH)

    depth = depth_of(128)
    group = lanes // SLAB
    for s in range(1, NT):
        now, later = CT.at[(s - 1) % 2], CT.at[s % 2]
        h = NT - 1 - s
        lo, hi = RC_ROWS - h, 2 * RC_ROWS + h
        for r in range(lo - 1, hi + 1):
            e = now[r, 0]
            total = (0.5 * CF[0]) * e
            for shift in range(1, L):
                total = total + (0.5 * CF[shift]) * pltpu.roll(e, shift, axis=0)
            PC[r] = total
        if s < NT - 1:
            arrived(s)
        for r in range(lo, hi):
            row = q * RC_ROWS + (r - RC_ROWS)
            f = rotation * (2.0 * (row.astype(F32) + 0.5) / (RC_ROWS * NL) - 1.0)
            inside = (row >= 0) & (row < RC_ROWS * NL)
            new = updated(now, r, PC, depth, WC[r], f, 2.0, None, (0.0, 1.0), STEPS * time_step, inside)
            for i in range(3):
                if RC_ROWS <= r < 2 * RC_ROWS:
                    RES[r - RC_ROWS, i] = new[i]
                if s < NT - 1:
                    later[r, i] = new[i] + row_of(s, r, i)
        for b in range(2):
            for i in range(3):
                packed = rolled(RES[4 * b, i], -16)
                for g in range(1, 4):
                    packed = jnp.where(group == g, rolled(RES[4 * b + g, i], SLAB * g - 16), packed)
                TC[s, b, i] = packed

        @pl.when(n != s)
        def _(s=s):
            result_copy(s).start()

        @pl.when(n == s)
        def _(s=s):
            RC[s] = TC[s]

    @pl.when(n > 0)
    def _():
        @pl.loop(1, NT)
        def _(j):
            result_arrival(lax.rem(n + j, NT)).wait_recv()

        for r in range(RC_ROWS):
            b, g = r // 4, r % 4
            for i in range(3):
                for j in range(WCO // 128):
                    value = rolled(RC[4 * j, b, i], -SLAB * g)
                    for m in range(1, 4):
                        value = jnp.where(group == m, rolled(RC[4 * j + m, b, i], SLAB * (m - g)), value)
                    CN[r, i, :, pl.ds(128 * j, 128)] = value

    coarse_new[...] = CN[...]
    keep.wait()
    for phase in range(2):
        for_deltas(phase, lambda copy: copy.wait_send())
        for s, d, there in passed_on(phase):
            @pl.when(there)
            def _(s=s, d=d, phase=phase):
                passing(s, d, phase).wait_send()
    for s in range(1, NT):
        @pl.when(n != s)
        def _(s=s):
            result_copy(s).wait_send()


def correct(state_in, coarse_in, old_in, ends, result, S, N, O, E, Q, WP, in_sem, out_sem):
    R, _, L, W = S.shape
    C, WCO = R // 2, W // 2
    fetches = []
    for f in range(3):
        for i, (source, target) in enumerate(((coarse_in.at[:, f], N.at[:, f]), (old_in.at[f], O.at[f]),
                                              (state_in.at[:, f], S.at[:, f]))):
            fetches.append(pltpu.make_async_copy(source, target, in_sem.at[f, i]))
            fetches[-1].start()
    WP[...] = jnp.where((iota((WCO, W), 1) >> 1) == iota((WCO, W), 0), 1.0, 0.0).astype(jnp.bfloat16)
    stores = []
    for f in range(3):
        fetches[3 * f].wait()
        fetches[3 * f + 1].wait()
        new = N[:, f]
        Q[f] = jnp.swapaxes(new, 0, 1)
        change = new - jnp.swapaxes(O[f], 0, 1)
        change = picked(change.reshape(C * L, WCO), WP[...]).reshape(C, L, W)
        fetches[3 * f + 2].wait()
        for b in range(R // 8):
            rows = jnp.stack([S[8 * b + i, f] + change[4 * b + i // 2] for i in range(8)])
            E[f, :, pl.ds(8 * b, 8), :] = jnp.swapaxes(rows, 0, 1)
        for i, (source, target) in enumerate(((E.at[f], ends.at[f]), (Q.at[f], result.at[f]))):
            stores.append(pltpu.make_async_copy(source, target, out_sem.at[f, i]))
            stores[-1].start()
    for store in stores:
        store.wait()


def local(NT, NL, starts, coarse_old, mean_depth, coupling, wet_cells):
    R, W = wet_cells.shape
    L = 8
    C, WCO = R // 2, W // 2
    E = R + 2 * HALO
    vmem = lambda *shape: pltpu.VMEM(shape, F32)
    half = lambda *shape: pltpu.VMEM(shape, jnp.bfloat16)
    sems = lambda *shape: pltpu.SemaphoreType.DMA(shape)
    space = pl.BlockSpec(memory_space=pltpu.VMEM)
    far = pl.BlockSpec(memory_space=pltpu.HBM)
    state, coarse_new = pl.pallas_call(
        functools.partial(kernel, NT, NL),
        out_shape=(jax.ShapeDtypeStruct((R, 3, L, W), F32), jax.ShapeDtypeStruct((C, 3, L, WCO), F32)),
        in_specs=[far] * 5,
        out_specs=(far, space),
        scratch_shapes=[
            vmem(3, L, R, W), vmem(3, L, C, WCO), vmem(L, L), pltpu.VMEM((R, W), jnp.int32), pltpu.SMEM((L,), F32),
            vmem(L, 128), vmem(L, L, 128), sems(8),
            vmem(E, 3, L, W), vmem(E, 3, L, W), vmem(E, 3, L, W), vmem(3, E, L, W), vmem(E, L, W),
            pltpu.VMEM((2, R, W), jnp.int32), vmem(STEPS, 2, HALO, 3, L, W),
            vmem(3 * C * L, 3 * C * L), vmem(3 * C * L, 3 * C * L),
            half(W, W), half(WCO, W), half(W, WCO), vmem(C, 3, L, W),
            vmem(NT, C // 2, 3, L, 128), vmem(NT - 1, 3 * C // 2, 3, L, 128),
            vmem(NT, 2, 3, L, 128), vmem(NT, 2, 3, L, 128),
            vmem(2, 3 * C, 3, L, 128), vmem(3 * C, L, 128), vmem(3 * C, L, 128), vmem(C, 3, L, 128),
            vmem(C, 3, L, WCO), vmem(C * 3 * L, W), vmem(C, 3, L, WCO),
            vmem(C + 2, 3, L, WCO), vmem(C + 2, L, WCO), vmem(C, L, WCO),
            sems(STEPS, 2, HALO), sems(STEPS, 2, HALO), sems(2), sems(2), sems(NT, 2), sems(NT - 1, 2), sems(NT - 1, 2, 2), sems(NT - 1, 2, 2), sems(NT), sems(NT),
        ],
        compiler_params=pltpu.CompilerParams(
            collective_id=0, has_side_effects=True, vmem_limit_bytes=63 * 1024 * 1024),
    )(starts[0], coarse_old[0], mean_depth, coupling, wet_cells)
    ends, result = pl.pallas_call(
        correct,
        out_shape=(jax.ShapeDtypeStruct((3, L, R, W), F32), jax.ShapeDtypeStruct((3, L, C, WCO), F32)),
        in_specs=[far] * 3,
        out_specs=(far, far),
        scratch_shapes=[
            vmem(R, 3, L, W), vmem(C, 3, L, WCO), vmem(3, L, C, WCO), vmem(3, L, R, W), vmem(3, L, C, WCO),
            half(WCO, W), sems(3, 3), sems(3, 2)],
        compiler_params=pltpu.CompilerParams(vmem_limit_bytes=63 * 1024 * 1024),
    )(state, coarse_new, coarse_old[0])
    return ends[None], result[None]


def solution(mesh):
    NT, NL = mesh.shape["tm"], mesh.shape["lat"]
    in_specs = (
        P("tm", None, None, "lat", None),
        P("tm", None, None, "lat", None),
        P(),
        P(),
        P("lat", None),
    )
    out_specs = (P("tm", None, None, "lat", None), P("tm", None, None, "lat", None))
    return jax.shard_map(functools.partial(local, NT, NL), mesh=mesh, in_specs=in_specs, out_specs=out_specs,
                         check_vma=False)
```

```python
import functools

import jax
import jax.numpy as jnp
from jax import lax
from jax.experimental import pallas as pl
from jax.experimental.pallas import tpu as pltpu
from jax.sharding import PartitionSpec as P

MESH = pl.DeviceIdType.MESH
F32 = jnp.float32

STEPS = 4
time_step = 0.15
viscosity = 0.02
rotation = 0.3

HALO = 3


def iota(shape, dim):
    return lax.broadcasted_iota(jnp.int32, shape, dim)


def dot(a, b):
    return jnp.dot(a, b, precision=lax.Precision.HIGHEST, preferred_element_type=F32)


def split(x, terms):
    parts = []
    for _ in range(terms):
        part = x.astype(jnp.bfloat16)
        parts.append(part)
        x = x - part.astype(F32)
    return parts


def picked(x, selector):
    rows = x.shape[0]
    result = jnp.dot(jnp.concatenate(split(x, 3), axis=0), selector, preferred_element_type=F32)
    return result[:rows] + (result[rows:2 * rows] + result[2 * rows:])


def mixed(matrix, x):
    high, low = split(matrix, 2)
    x_high, x_low = split(x, 2)
    product = lambda a, b: jnp.dot(a, b, preferred_element_type=F32)
    return product(high, x_high) + (product(high, x_low) + product(low, x_high))


def widened(x, width):
    return x if width == x.shape[1] else jnp.concatenate([x] * (width // x.shape[1]), axis=1)


def rolled(x, shift):
    return pltpu.roll(x, shift % x.shape[-1], axis=x.ndim - 1)


def updated(src, r, p, depth, wet, f, spacing, old, weights, step, inside):
    k = viscosity / (spacing * spacing)
    half = 0.5 / spacing
    e, u, v = src[r, 0], src[r, 1], src[r, 2]
    un, us = src[r + 1, 1], src[r - 1, 1]
    vn, vs = src[r + 1, 2], src[r - 1, 2]
    hvn = (depth + src[r + 1, 0]) * vn
    hvs = (depth + src[r - 1, 0]) * vs
    hu = (depth + e) * u
    pc = p[r]
    ue, uw = rolled(u, -1), rolled(u, 1)
    ve, vw = rolled(v, -1), rolled(v, 1)
    u2, v2 = u * half, v * half
    east, west, north, south = k - u2, k + u2, k - v2, k + v2
    zu = (ue * east + uw * west) + (un * north + us * south)
    zv = (ve * east + vw * west) + (vn * north + vs * south)
    zu = zu + (f * v - (4.0 * k) * u) - (rolled(pc, -1) - rolled(pc, 1))
    zv = zv - (f * u + (4.0 * k) * v) - (p[r + 1] - p[r - 1])
    ze = (rolled(hu, -1) - rolled(hu, 1)) + (hvn - hvs)
    w = wet * step
    ce = jnp.where(inside, -step * half, 0.0).astype(F32)
    out = [ce * ze, w * zu, w * zv]
    first, second = weights
    now = [e, u, v]
    for i in range(3):
        out[i] = out[i] + (now[i] if second == 1.0 else second * now[i])
        if first != 0.0:
            out[i] = out[i] + first * old[r, i]
    return out


def kernel(NT, NL, starts_in, old_in, depth_in, coupling_in, wet_in, ends, RC,
           SV, OV, CV, WV, DS, DP, CF, in_sem, YA, Y1, Y2, PB, WET, WX, HB, KF, KC, WW, W2, WR, DL, TX, RX, TC, PK, CT, PC, WC, RES,
           CO, BW, CN, C0, P0, W0,
           hs_send, hs_recv, wx_send, wx_recv, tx_send, rx_recv, fw_send, fw_recv, tc_send, rc_recv):
    starts, coarse_old, mean_depth, coupling, wet_cells = SV, OV, DS, CV, WV
    R, W = wet_cells.shape
    L = 8
    fetches = [pltpu.make_async_copy(source, target, in_sem.at[i]) for i, (source, target) in enumerate(
        [(starts_in.at[f], SV.at[f]) for f in range(3)] + [(wet_in, WV), (coupling_in, CV), (depth_in, DS), (old_in, OV)])]
    for fetch in fetches:
        fetch.start()
    RC_ROWS, WCO = R // 2, W // 2
    SLAB = WCO // NT
    n, q = lax.axis_index("tm"), lax.axis_index("lat")
    up, down = q > 0, q < NL - 1
    inside_side = {-1: up, 1: down}

    barrier = pltpu.get_barrier_semaphore()

    def greet(m, row):
        pl.semaphore_signal(barrier, inc=1, device_id=(m, row), device_id_type=MESH)

    for j in range(1, NT):
        greet(lax.rem(n + j, NT), q)
    for d in (-1, 1):
        @pl.when(inside_side[d])
        def _(d=d):
            greet(n, q + d)

    pl.semaphore_wait(barrier, (NT - 1) + up.astype(jnp.int32) + down.astype(jnp.int32))
    for f in range(3):
        fetches[f].wait()
        for b in range(R // 8):
            YA[pl.ds(HALO + 8 * b, 8), f] = jnp.swapaxes(starts[f, :, pl.ds(8 * b, 8), :], 0, 1)
        for side in (-1, 1):
            @pl.when(inside_side[side])
            def _(f=f, side=side):
                slot = 1 if side == -1 else 0
                pltpu.make_async_remote_copy(
                    src_ref=YA.at[pl.ds(HALO if side == -1 else R, HALO), f], dst_ref=HB.at[0, slot, :, f],
                    send_sem=hs_send.at[0, slot, f], recv_sem=hs_recv.at[0, slot, f],
                    device_id=(n, q + side), device_id_type=MESH).start()


    def halo_copy(k, side, j):
        row = HALO + HALO - 1 - j if side == -1 else R + j
        slot = 1 if side == -1 else 0
        return pltpu.make_async_remote_copy(
            src_ref=YA.at[row], dst_ref=HB.at[k, slot, row - HALO if side == -1 else j],
            send_sem=hs_send.at[k, slot, j], recv_sem=hs_recv.at[k, slot, j],
            device_id=(n, q + side), device_id_type=MESH)

    def halo_arrival(k, side, j):
        slot = 0 if side == -1 else 1
        return pltpu.make_async_remote_copy(
            src_ref=YA.at[0], dst_ref=HB.at[k, slot, j if side == -1 else HALO - 1 - j],
            send_sem=hs_send.at[k, slot, j], recv_sem=hs_recv.at[k, slot, j],
            device_id=(n, q + side), device_id_type=MESH)

    def wet_copy(side):
        slot = 1 if side == -1 else 0
        return pltpu.make_async_remote_copy(
            src_ref=wet_cells, dst_ref=WX.at[slot], send_sem=wx_send.at[slot], recv_sem=wx_recv.at[slot],
            device_id=(n, q + side), device_id_type=MESH)

    def send_row(k, j):
        for side in (-1, 1):
            @pl.when(inside_side[side])
            def _(side=side):
                halo_copy(k, side, j).start()

    for fetch in fetches[3:]:
        fetch.wait()
    for side in (-1, 1):
        @pl.when(inside_side[side])
        def _(side=side):
            wet_copy(side).start()

        @pl.when(jnp.logical_not(inside_side[side]))
        def _(side=side):
            slot = 0 if side == -1 else 1
            WX[slot] = jnp.zeros((R, W), jnp.int32)
            YA[pl.ds(0 if side == -1 else HALO + R, HALO)] = jnp.zeros((HALO, 3, L, W), F32)
            RX[:, pl.ds(0 if side == -1 else RC_ROWS, RC_ROWS // 2)] = jnp.zeros(
                (NT - 1, RC_ROWS // 2, 3, L, 128), F32)

    KN = KF.shape[0]
    spread = (iota((KN, L), 0) % L == iota((KN, L), 1)).astype(F32)
    spread_t = (iota((L, KN), 1) % L == iota((L, KN), 0)).astype(F32)
    blocks = dot(dot(spread, coupling[...]), spread_t)
    blocks = jnp.where(iota((KN, KN), 0) // L == iota((KN, KN), 1) // L, blocks, 0.0)
    KF[...] = 0.5 * blocks
    KC[...] = 0.25 * blocks
    for shift in range(L):
        column = (iota((L, L), 0) - shift + L) & (L - 1)
        part = jnp.sum(jnp.where(iota((L, L), 1) == column, coupling[...], 0.0), axis=1, keepdims=True)
        CF[shift] = jnp.broadcast_to(0.5 * part, (L, 128))

    layer = iota((L, 128), 0)
    value = jnp.zeros((L, 128), F32)
    for l in range(L):
        value = jnp.where(layer == l, mean_depth[l], value)
    DP[...] = value

    def depth_of(width):
        return widened(DP[...], width)

    wet_own = wet_cells[...].astype(F32)
    for r in range(R):
        WET[HALO + r] = jnp.broadcast_to(wet_own[r:r + 1, :], (L, W))

    position = iota((8, W), 1)
    target = ((position >> 6) * SLAB - 16 + (position & 63)) & (WCO - 1)
    target = target[:1]
    selector = lambda where: jnp.where(where, 1.0, 0.0).astype(jnp.bfloat16)
    WW[...] = selector((iota((W, W), 0) >> 1) == target)
    W2[...] = selector(iota((WCO, W), 0) == target)
    WR[...] = selector((iota((W, WCO), 0) >> 1) == iota((W, WCO), 1))

    @pl.when(n == 0)
    def _():
        sums = jnp.stack([YA[HALO + 2 * i] + YA[HALO + 1 + 2 * i] for i in range(RC_ROWS)])
        C0[pl.ds(1, RC_ROWS)] = (0.25 * picked(sums.reshape(-1, W), WR[...])).reshape(RC_ROWS, 3, L, WCO)

    for f in range(3):
        CO[:, f] = jnp.swapaxes(coarse_old[f], 0, 1)

    def fine_f(r):
        row = q * R + (r - HALO)
        return rotation * (2.0 * (row.astype(F32) + 0.5) / (R * NL) - 1.0), (row >= 0) & (row < R * NL)

    stages = (
        (YA, Y1, (0.0, 1.0), 1.0),
        (Y1, Y2, (0.75, 0.25), 0.25),
        (Y2, YA, (1.0 / 3.0, 2.0 / 3.0), 2.0 / 3.0),
    )

    def pressure(stage, pieces):
        src = stages[stage][0]
        count = sum(c for _, c in pieces)
        rows = [src[pl.ds(a, c), 0] for a, c in pieces]
        rows = rows[0] if len(rows) == 1 else jnp.concatenate(rows, axis=0)
        size = count * L
        result = mixed(KF[pl.ds(0, size), pl.ds(0, size)], rows.reshape(size, W)).reshape(count, L, W)
        at = 0
        for a, c in pieces:
            PB[stage, pl.ds(a, c)] = result[at:at + c]
            at += c

    def row_pressure(stage, r):
        e = stages[stage][0][r, 0]
        total = widened(CF[0], W) * e
        for shift in range(1, L):
            total = total + widened(CF[shift], W) * pltpu.roll(e, shift, axis=0)
        PB[stage, r] = total

    def fine_row(stage, r):
        src, dst, weights, g = stages[stage]
        f, inside = fine_f(r)
        new = updated(src, r, PB.at[stage], depth_of(W), WET[r], f, 1.0, YA, weights, g * time_step, inside)
        for i in range(3):
            dst[r, i] = new[i]

    def coarse_first():
        sums = jnp.stack([YA[1] + YA[2], YA[HALO + R] + YA[HALO + R + 1]])
        outer = (0.25 * picked(sums.reshape(-1, W), WR[...])).reshape(2, 3, L, WCO)
        C0[0] = outer[0]
        C0[RC_ROWS + 1] = outer[1]
        size = (RC_ROWS + 2) * L
        P0[...] = mixed(KC[pl.ds(0, size), pl.ds(0, size)], C0[:, 0].reshape(size, WCO)).reshape(RC_ROWS + 2, L, WCO)
        pairs = (iota((RC_ROWS, R), 1) // 2 == iota((RC_ROWS, R), 0)).astype(F32)
        wet_full = (jnp.dot(jnp.dot(pairs, wet_cells[...].astype(F32)), WR[...].astype(F32)) > 3.5).astype(F32)
        for i in range(RC_ROWS):
            W0[i] = jnp.broadcast_to(wet_full[i:i + 1, :], (L, WCO))

        @pl.loop(1, RC_ROWS + 1)
        def _(r):
            row = q * RC_ROWS + r - 1
            f = rotation * (2.0 * (row.astype(F32) + 0.5) / (RC_ROWS * NL) - 1.0)
            new = updated(C0, r, P0, depth_of(WCO), W0[r - 1], f, 2.0, None, (0.0, 1.0), STEPS * time_step, True)
            for i in range(3):
                CN[r - 1, i] = new[i]

    HU = RC_ROWS // 2
    lanes = iota((L, 128), 1)
    group = lanes // SLAB

    def side_by_side(parts):
        packed = parts[0]
        for g in range(1, 4):
            packed = jnp.where(group == g, parts[g], packed)
        return packed

    def own_result(source):
        return pltpu.make_async_copy(source, RC.at[n], in_sem.at[8])

    def first_result():
        return pltpu.make_async_copy(PK, RC, in_sem.at[8])

    def slot_of(unit):
        return {1: 0, 2: 1, 0: 2, 3: 3}[unit]

    def deltas(units):
        rows = [2 * unit + more for unit in units for more in range(2)]
        sums = jnp.stack([YA[HALO + 2 * i] + YA[HALO + 1 + 2 * i] for i in rows])
        change = (0.25 * picked(sums.reshape(-1, W), WW[...])).reshape(len(rows), 3, L, W)
        for at, i in enumerate(rows):
            DL[i] = change[at] + BW[pl.ds(i * 3 * L, 3 * L)].reshape(3, L, W)
        for i in units:
            for f in range(3):
                for j in range(NT // 2):
                    a = DL[2 * i, f, :, pl.ds(128 * j, 128)]
                    b = DL[2 * i + 1, f, :, pl.ds(128 * j, 128)]
                    TX[2 * j, slot_of(i), f] = jnp.where(lanes < 64, a, rolled(b, 64))
                    TX[2 * j + 1, slot_of(i), f] = jnp.where(lanes < 64, rolled(a, 64), b)

    def piece(d, phase, units):
        if d == 0 or units == 4:
            return 2 * phase, 2
        if phase == 1:
            return (3 if d == 1 else 2), 1
        return {1: (0, 0), 2: (1 if d == 1 else 0, 1), 3: (0, 2)}[units]

    def delta_copy(m, phase):
        return pltpu.make_async_remote_copy(
            src_ref=TX.at[m, pl.ds(2 * phase, 2)], dst_ref=RX.at[n, pl.ds(HU + 2 * phase, 2)],
            send_sem=tx_send.at[m, phase], recv_sem=rx_recv.at[n, phase],
            device_id=(m, q), device_id_type=MESH)

    def delta_arrival(s, phase):
        return pltpu.make_async_remote_copy(
            src_ref=TX.at[0, pl.ds(0, 2)], dst_ref=RX.at[s, pl.ds(HU + 2 * phase, 2)],
            send_sem=tx_send.at[0, phase], recv_sem=rx_recv.at[s, phase],
            device_id=(s, q), device_id_type=MESH)

    def for_deltas(phase, act):
        @pl.when(n < NT - 1)
        def _():
            @pl.loop(1, NT)
            def _(j):
                act(delta_copy(lax.rem(n + j, NT), phase))

    def send_deltas(phase):
        for_deltas(phase, lambda copy: copy.start())

        @pl.when(n < NT - 1)
        def _():
            RX[n, pl.ds(HU + 2 * phase, 2)] = TX[n, pl.ds(2 * phase, 2)]

    def passing(s, d, phase):
        first, count = piece(d, phase, (NT - s) // 2)
        side = 0 if d == 1 else 1
        return pltpu.make_async_remote_copy(
            src_ref=RX.at[s, pl.ds(HU + first, count)], dst_ref=RX.at[s, pl.ds(HU * (1 - d) + first, count)],
            send_sem=fw_send.at[s, side, phase], recv_sem=fw_recv.at[s, side, phase],
            device_id=(n, q + d), device_id_type=MESH)

    def passed_on(phase):
        return [(s, d, there) for s in range(NT - 1) for d, there in ((1, down), (-1, up))
                if piece(d, phase, (NT - s) // 2)[1]]

    def pass_deltas(phase):
        for s in range(NT - 1):
            @pl.when(n != s)
            def _(s=s):
                delta_arrival(s, phase).wait_recv()
            for t, d, there in passed_on(phase):
                if t == s:
                    @pl.when(there)
                    def _(s=s, d=d):
                        passing(s, d, phase).start()

    @pl.loop(0, STEPS)
    def _(k):
        for stage in range(3):
            pressure(stage, [(HALO + stage, R - 2 * stage)])

            for r in range(R - 2 * (stage + 1)):
                fine_row(stage, HALO + stage + 1 + r)

        @pl.when(k == STEPS - 1)
        def _():
            deltas((1, 2))
            send_deltas(0)

        for side in (-1, 1):
            slot = 0 if side == -1 else 1

            @pl.when(inside_side[side])
            def _(side=side, slot=slot):
                for j in range(HALO):
                    halo_arrival(k, side, j).wait_recv()
                YA[pl.ds(0 if side == -1 else HALO + R, HALO)] = HB[k, slot]
                for j in range(HALO):
                    halo_copy(k, side, j).wait_send()

        @pl.when(k == 0)
        def _():
            for side in (-1, 1):
                @pl.when(inside_side[side])
                def _(side=side):
                    wet_copy(side).wait_send()
                    wet_copy(-side).wait_recv()
            for r in range(HALO):
                WET[r] = jnp.broadcast_to(WX[0, R - HALO + r:R - HALO + r + 1, :].astype(F32), (L, W))
                WET[HALO + R + r] = jnp.broadcast_to(WX[1, r:r + 1, :].astype(F32), (L, W))

        for j in range(HALO):
            for stage in range(3):
                low, high = HALO - j + stage, HALO + R - 1 + j - stage
                row_pressure(stage, low - 1)
                row_pressure(stage, high + 1)
                fine_row(stage, low)
                fine_row(stage, high)

            @pl.when(k < STEPS - 1)
            def _(j=j):
                send_row(k + 1, j)

        @pl.when(k == 0)
        def _():
            @pl.when(n == 0)
            def _():
                coarse_first()
                for m in range(NT):
                    at = SLAB * m // 128 * 128
                    for b in range(2):
                        for i in range(3):
                            PK[m, b, i] = side_by_side([
                                rolled(CN[4 * b + g, i, :, pl.ds(at, 128)], SLAB * g - (SLAB * m - at)) for g in range(4)])
                first_result().start()
                BW[...] = picked((CN[...] - CO[...]).reshape(-1, WCO), W2[...])

            @pl.when(n > 0)
            def _():
                BW[...] = picked((-CO[...]).reshape(-1, WCO), W2[...])

    keep = pltpu.make_async_copy(YA.at[pl.ds(HALO, R)], ends, in_sem.at[5 + 2])
    keep.start()
    deltas((0, 3))
    send_deltas(1)
    pass_deltas(0)

    E = 3 * RC_ROWS
    col = iota((W, 128), 1)
    own = (n * SLAB - 16 + col) & (WCO - 1)
    picks = jnp.where(((iota((W, 128), 0) >> 1) == own) & (col < 64), 1.0, 0.0).astype(F32)
    pairs = (iota((RC_ROWS, R), 1) // 2 == iota((RC_ROWS, R), 0)).astype(F32)
    for part, cells in enumerate((WX[0], wet_cells[...], WX[1])):
        window = (jnp.dot(jnp.dot(pairs, cells.astype(F32)), picks) > 3.5).astype(F32)
        for i in range(RC_ROWS):
            WC[part * RC_ROWS + i] = jnp.broadcast_to(window[i:i + 1, :], (L, 128))

    pass_deltas(1)

    def arrived(s):
        for phase in range(2):
            for t, d, _ in passed_on(phase):
                if t == s:
                    @pl.when(up if d == 1 else down)
                    def _(d=d, phase=phase):
                        passing(s, d, phase).wait_recv()

    def row_of(s, r, f):
        x = RX[s, r // 2 // HU * HU + slot_of(r // 2 % HU), f]
        return x if r % 2 == 0 else rolled(x, 64)

    arrived(0)
    for r in range(E):
        for f in range(3):
            CT[0, r, f] = row_of(0, r, f)

    def result_copy(s):
        return pltpu.make_async_remote_copy(
            src_ref=TC.at[s], dst_ref=RC.at[n], send_sem=tc_send.at[s], recv_sem=rc_recv.at[n],
            device_id=(s, q), device_id_type=MESH)

    def result_arrival(m):
        return pltpu.make_async_remote_copy(
            src_ref=TC.at[0], dst_ref=RC.at[m], send_sem=tc_send.at[0], recv_sem=rc_recv.at[m],
            device_id=(m, q), device_id_type=MESH)

    depth = depth_of(128)
    for s in range(1, NT):
        now, later = CT.at[(s - 1) % 2], CT.at[s % 2]
        h = NT - 1 - s
        lo, hi = RC_ROWS - h, 2 * RC_ROWS + h
        for r in range(lo - 1, hi + 1):
            e = now[r, 0]
            total = (0.5 * CF[0]) * e
            for shift in range(1, L):
                total = total + (0.5 * CF[shift]) * pltpu.roll(e, shift, axis=0)
            PC[r] = total
        if s < NT - 1:
            arrived(s)
        for r in range(lo, hi):
            row = q * RC_ROWS + (r - RC_ROWS)
            f = rotation * (2.0 * (row.astype(F32) + 0.5) / (RC_ROWS * NL) - 1.0)
            inside = (row >= 0) & (row < RC_ROWS * NL)
            new = updated(now, r, PC, depth, WC[r], f, 2.0, None, (0.0, 1.0), STEPS * time_step, inside)
            for i in range(3):
                if RC_ROWS <= r < 2 * RC_ROWS:
                    RES[r - RC_ROWS, i] = new[i]
                if s < NT - 1:
                    later[r, i] = new[i] + row_of(s, r, i)
        for b in range(2):
            for i in range(3):
                TC[s, b, i] = side_by_side([rolled(RES[4 * b + g, i], SLAB * g - 16) for g in range(4)])

        @pl.when(n != s)
        def _(s=s):
            result_copy(s).start()

        @pl.when(n == s)
        def _(s=s):
            own_result(TC.at[s]).start()

    @pl.when(n > 0)
    def _():
        @pl.loop(1, NT)
        def _(j):
            result_arrival(lax.rem(n + j, NT)).wait_recv()

        own_result(TC.at[n]).wait()

    @pl.when(n == 0)
    def _():
        first_result().wait()

    keep.wait()
    for phase in range(2):
        for_deltas(phase, lambda copy: copy.wait_send())
        for s, d, there in passed_on(phase):
            @pl.when(there)
            def _(s=s, d=d, phase=phase):
                passing(s, d, phase).wait_send()
    for s in range(1, NT):
        @pl.when(n != s)
        def _(s=s):
            result_copy(s).wait_send()


def correct(state_in, coarse_in, old_in, ends, result, S, N, O, E, Q, WP, in_sem, out_sem):
    R, _, L, W = S.shape
    C, WCO = R // 2, W // 2
    SLAB = WCO // N.shape[0]
    group = iota((L, 128), 1) // SLAB
    fetches = []
    for f in range(3):
        for i, (source, target) in enumerate(((coarse_in.at[:, :, f], N.at[:, :, f]), (old_in.at[f], O.at[f]),
                                              (state_in.at[:, f], S.at[:, f]))):
            fetches.append(pltpu.make_async_copy(source, target, in_sem.at[f, i]))
            fetches[-1].start()
    WP[...] = jnp.where((iota((WCO, W), 1) >> 1) == iota((WCO, W), 0), 1.0, 0.0).astype(jnp.bfloat16)
    stores = []
    for f in range(3):
        fetches[3 * f].wait()
        fetches[3 * f + 1].wait()
        rows = []
        for r in range(C):
            parts = []
            for j in range(WCO // 128):
                value = rolled(N[4 * j, r // 4, f], -SLAB * (r % 4))
                for m in range(1, 4):
                    value = jnp.where(group == m, rolled(N[4 * j + m, r // 4, f], SLAB * (m - r % 4)), value)
                parts.append(value)
            rows.append(jnp.concatenate(parts, axis=1))
        new = jnp.stack(rows)
        Q[f] = jnp.swapaxes(new, 0, 1)
        change = new - jnp.swapaxes(O[f], 0, 1)
        change = picked(change.reshape(C * L, WCO), WP[...]).reshape(C, L, W)
        fetches[3 * f + 2].wait()
        for b in range(R // 8):
            rows = jnp.stack([S[8 * b + i, f] + change[4 * b + i // 2] for i in range(8)])
            E[f, :, pl.ds(8 * b, 8), :] = jnp.swapaxes(rows, 0, 1)
        for i, (source, target) in enumerate(((E.at[f], ends.at[f]), (Q.at[f], result.at[f]))):
            stores.append(pltpu.make_async_copy(source, target, out_sem.at[f, i]))
            stores[-1].start()
    for store in stores:
        store.wait()


def local(NT, NL, starts, coarse_old, mean_depth, coupling, wet_cells):
    R, W = wet_cells.shape
    L = 8
    C, WCO = R // 2, W // 2
    E = R + 2 * HALO
    vmem = lambda *shape: pltpu.VMEM(shape, F32)
    half = lambda *shape: pltpu.VMEM(shape, jnp.bfloat16)
    sems = lambda *shape: pltpu.SemaphoreType.DMA(shape)
    far = pl.BlockSpec(memory_space=pltpu.HBM)
    state, coarse_new = pl.pallas_call(
        functools.partial(kernel, NT, NL),
        out_shape=(jax.ShapeDtypeStruct((R, 3, L, W), F32), jax.ShapeDtypeStruct((NT, 2, 3, L, 128), F32)),
        in_specs=[far] * 5,
        out_specs=(far, far),
        scratch_shapes=[
            vmem(3, L, R, W), vmem(3, L, C, WCO), vmem(L, L), pltpu.VMEM((R, W), jnp.int32), pltpu.SMEM((L,), F32),
            vmem(L, 128), vmem(L, L, 128), sems(9),
            vmem(E, 3, L, W), vmem(E, 3, L, W), vmem(E, 3, L, W), vmem(3, E, L, W), vmem(E, L, W),
            pltpu.VMEM((2, R, W), jnp.int32), vmem(STEPS, 2, HALO, 3, L, W),
            vmem(3 * C * L, 3 * C * L), vmem(3 * C * L, 3 * C * L),
            half(W, W), half(WCO, W), half(W, WCO), vmem(C, 3, L, W),
            vmem(NT, C // 2, 3, L, 128), vmem(NT - 1, 3 * C // 2, 3, L, 128),
            vmem(NT, 2, 3, L, 128), vmem(NT, 2, 3, L, 128),
            vmem(2, 3 * C, 3, L, 128), vmem(3 * C, L, 128), vmem(3 * C, L, 128), vmem(C, 3, L, 128),
            vmem(C, 3, L, WCO), vmem(C * 3 * L, W), vmem(C, 3, L, WCO),
            vmem(C + 2, 3, L, WCO), vmem(C + 2, L, WCO), vmem(C, L, WCO),
            sems(STEPS, 2, HALO), sems(STEPS, 2, HALO), sems(2), sems(2), sems(NT, 2), sems(NT - 1, 2), sems(NT - 1, 2, 2), sems(NT - 1, 2, 2), sems(NT), sems(NT),
        ],
        compiler_params=pltpu.CompilerParams(
            collective_id=0, has_side_effects=True, vmem_limit_bytes=63 * 1024 * 1024),
    )(starts[0], coarse_old[0], mean_depth, coupling, wet_cells)
    ends, result = pl.pallas_call(
        correct,
        out_shape=(jax.ShapeDtypeStruct((3, L, R, W), F32), jax.ShapeDtypeStruct((3, L, C, WCO), F32)),
        in_specs=[far] * 3,
        out_specs=(far, far),
        scratch_shapes=[
            vmem(R, 3, L, W), vmem(NT, 2, 3, L, 128), vmem(3, L, C, WCO), vmem(3, L, R, W), vmem(3, L, C, WCO),
            half(WCO, W), sems(3, 3), sems(3, 2)],
        compiler_params=pltpu.CompilerParams(vmem_limit_bytes=63 * 1024 * 1024),
    )(state, coarse_new, coarse_old[0])
    return ends[None], result[None]


def solution(mesh):
    NT, NL = mesh.shape["tm"], mesh.shape["lat"]
    in_specs = (
        P("tm", None, None, "lat", None),
        P("tm", None, None, "lat", None),
        P(),
        P(),
        P("lat", None),
    )
    out_specs = (P("tm", None, None, "lat", None), P("tm", None, None, "lat", None))
    return jax.shard_map(functools.partial(local, NT, NL), mesh=mesh, in_specs=in_specs, out_specs=out_specs,
                         check_vma=False)
```

```python
import functools

import jax
import jax.numpy as jnp
from jax import lax
from jax.experimental import pallas as pl
from jax.experimental.pallas import tpu as pltpu
from jax.sharding import PartitionSpec as P

MESH = pl.DeviceIdType.MESH
F32 = jnp.float32

STEPS = 4
time_step = 0.15
viscosity = 0.02
rotation = 0.3

HALO = 3


def iota(shape, dim):
    return lax.broadcasted_iota(jnp.int32, shape, dim)


def dot(a, b):
    return jnp.dot(a, b, precision=lax.Precision.HIGHEST, preferred_element_type=F32)


def split(x, terms):
    parts = []
    for _ in range(terms):
        part = x.astype(jnp.bfloat16)
        parts.append(part)
        x = x - part.astype(F32)
    return parts


def picked(x, selector):
    rows = x.shape[0]
    result = jnp.dot(jnp.concatenate(split(x, 3), axis=0), selector, preferred_element_type=F32)
    return result[:rows] + (result[rows:2 * rows] + result[2 * rows:])


def mixed(matrix, x):
    high, low = split(matrix, 2)
    x_high, x_low = split(x, 2)
    product = lambda a, b: jnp.dot(a, b, preferred_element_type=F32)
    return product(high, x_high) + (product(high, x_low) + product(low, x_high))


def widened(x, width):
    return x if width == x.shape[1] else jnp.concatenate([x] * (width // x.shape[1]), axis=1)


def rolled(x, shift):
    return pltpu.roll(x, shift % x.shape[-1], axis=x.ndim - 1)


def updated(src, r, p, depth, wet, f, spacing, old, weights, step, inside):
    k = viscosity / (spacing * spacing)
    half = 0.5 / spacing
    e, u, v = src[r, 0], src[r, 1], src[r, 2]
    un, us = src[r + 1, 1], src[r - 1, 1]
    vn, vs = src[r + 1, 2], src[r - 1, 2]
    hvn = (depth + src[r + 1, 0]) * vn
    hvs = (depth + src[r - 1, 0]) * vs
    hu = (depth + e) * u
    pc = p[r]
    ue, uw = rolled(u, -1), rolled(u, 1)
    ve, vw = rolled(v, -1), rolled(v, 1)
    u2, v2 = u * half, v * half
    east, west, north, south = k - u2, k + u2, k - v2, k + v2
    zu = (ue * east + uw * west) + (un * north + us * south)
    zv = (ve * east + vw * west) + (vn * north + vs * south)
    zu = zu + (f * v - (4.0 * k) * u) - (rolled(pc, -1) - rolled(pc, 1))
    zv = zv - (f * u + (4.0 * k) * v) - (p[r + 1] - p[r - 1])
    ze = (rolled(hu, -1) - rolled(hu, 1)) + (hvn - hvs)
    w = wet * step
    ce = jnp.where(inside, -step * half, 0.0).astype(F32)
    out = [ce * ze, w * zu, w * zv]
    first, second = weights
    now = [e, u, v]
    for i in range(3):
        out[i] = out[i] + (now[i] if second == 1.0 else second * now[i])
        if first != 0.0:
            out[i] = out[i] + first * old[r, i]
    return out


def kernel(NT, NL, starts_in, old_in, depth_in, coupling_in, wet_in, ends, RC,
           SV, OV, CV, WV, DS, DP, CF, in_sem, YA, Y1, Y2, PB, WET, WX, HB, KF, KC, WW, W2, WR, DL, TX, RX, TC, PK, CT, PC, WC, RES,
           CO, BW, CN, C0, P0, W0,
           hs_send, hs_recv, wx_send, wx_recv, tx_send, rx_recv, fw_send, fw_recv, tc_send, rc_recv):
    starts, coarse_old, mean_depth, coupling, wet_cells = SV, OV, DS, CV, WV
    R, W = wet_cells.shape
    L = 8
    fetches = [pltpu.make_async_copy(source, target, in_sem.at[i]) for i, (source, target) in enumerate(
        [(starts_in.at[f], SV.at[f]) for f in range(3)] + [(wet_in, WV), (coupling_in, CV), (depth_in, DS), (old_in, OV)])]
    for fetch in fetches:
        fetch.start()
    RC_ROWS, WCO = R // 2, W // 2
    SLAB = WCO // NT
    n, q = lax.axis_index("tm"), lax.axis_index("lat")
    up, down = q > 0, q < NL - 1
    inside_side = {-1: up, 1: down}

    barrier = pltpu.get_barrier_semaphore()

    def greet(m, row):
        pl.semaphore_signal(barrier, inc=1, device_id=(m, row), device_id_type=MESH)

    for j in range(1, NT):
        greet(lax.rem(n + j, NT), q)
    for d in (-1, 1):
        @pl.when(inside_side[d])
        def _(d=d):
            greet(n, q + d)

    pl.semaphore_wait(barrier, (NT - 1) + up.astype(jnp.int32) + down.astype(jnp.int32))
    for f in range(3):
        fetches[f].wait()
        for b in range(R // 8):
            YA[pl.ds(HALO + 8 * b, 8), f] = jnp.swapaxes(starts[f, :, pl.ds(8 * b, 8), :], 0, 1)
        for side in (-1, 1):
            @pl.when(inside_side[side])
            def _(f=f, side=side):
                slot = 1 if side == -1 else 0
                pltpu.make_async_remote_copy(
                    src_ref=YA.at[pl.ds(HALO if side == -1 else R, HALO), f], dst_ref=HB.at[0, slot, :, f],
                    send_sem=hs_send.at[0, slot, f], recv_sem=hs_recv.at[0, slot, f],
                    device_id=(n, q + side), device_id_type=MESH).start()


    def halo_copy(k, side, j):
        row = HALO + HALO - 1 - j if side == -1 else R + j
        slot = 1 if side == -1 else 0
        return pltpu.make_async_remote_copy(
            src_ref=YA.at[row], dst_ref=HB.at[k, slot, row - HALO if side == -1 else j],
            send_sem=hs_send.at[k, slot, j], recv_sem=hs_recv.at[k, slot, j],
            device_id=(n, q + side), device_id_type=MESH)

    def halo_arrival(k, side, j):
        slot = 0 if side == -1 else 1
        return pltpu.make_async_remote_copy(
            src_ref=YA.at[0], dst_ref=HB.at[k, slot, j if side == -1 else HALO - 1 - j],
            send_sem=hs_send.at[k, slot, j], recv_sem=hs_recv.at[k, slot, j],
            device_id=(n, q + side), device_id_type=MESH)

    def wet_copy(side):
        slot = 1 if side == -1 else 0
        return pltpu.make_async_remote_copy(
            src_ref=wet_cells, dst_ref=WX.at[slot], send_sem=wx_send.at[slot], recv_sem=wx_recv.at[slot],
            device_id=(n, q + side), device_id_type=MESH)

    def send_row(k, j):
        for side in (-1, 1):
            @pl.when(inside_side[side])
            def _(side=side):
                halo_copy(k, side, j).start()

    for fetch in fetches[3:]:
        fetch.wait()
    for side in (-1, 1):
        @pl.when(inside_side[side])
        def _(side=side):
            wet_copy(side).start()

        @pl.when(jnp.logical_not(inside_side[side]))
        def _(side=side):
            slot = 0 if side == -1 else 1
            WX[slot] = jnp.zeros((R, W), jnp.int32)
            YA[pl.ds(0 if side == -1 else HALO + R, HALO)] = jnp.zeros((HALO, 3, L, W), F32)
            RX[:, pl.ds(0 if side == -1 else RC_ROWS, RC_ROWS // 2)] = jnp.zeros(
                (NT - 1, RC_ROWS // 2, 3, L, 128), F32)

    KN = KF.shape[0]
    spread = (iota((KN, L), 0) % L == iota((KN, L), 1)).astype(F32)
    spread_t = (iota((L, KN), 1) % L == iota((L, KN), 0)).astype(F32)
    blocks = dot(dot(spread, coupling[...]), spread_t)
    blocks = jnp.where(iota((KN, KN), 0) // L == iota((KN, KN), 1) // L, blocks, 0.0)
    KF[...] = 0.5 * blocks
    KC[...] = 0.25 * blocks
    for shift in range(L):
        column = (iota((L, L), 0) - shift + L) & (L - 1)
        part = jnp.sum(jnp.where(iota((L, L), 1) == column, coupling[...], 0.0), axis=1, keepdims=True)
        CF[shift] = jnp.broadcast_to(0.5 * part, (L, 128))

    layer = iota((L, 128), 0)
    value = jnp.zeros((L, 128), F32)
    for l in range(L):
        value = jnp.where(layer == l, mean_depth[l], value)
    DP[...] = value

    def depth_of(width):
        return widened(DP[...], width)

    wet_own = wet_cells[...].astype(F32)
    for r in range(R):
        WET[HALO + r] = jnp.broadcast_to(wet_own[r:r + 1, :], (L, W))

    position = iota((8, W), 1)
    target = ((position >> 6) * SLAB - 16 + (position & 63)) & (WCO - 1)
    target = target[:1]
    selector = lambda where: jnp.where(where, 1.0, 0.0).astype(jnp.bfloat16)
    WW[...] = selector((iota((W, W), 0) >> 1) == target)
    W2[...] = selector(iota((WCO, W), 0) == target)
    WR[...] = selector((iota((W, WCO), 0) >> 1) == iota((W, WCO), 1))

    @pl.when(n == 0)
    def _():
        sums = jnp.stack([YA[HALO + 2 * i] + YA[HALO + 1 + 2 * i] for i in range(RC_ROWS)])
        C0[pl.ds(1, RC_ROWS)] = (0.25 * picked(sums.reshape(-1, W), WR[...])).reshape(RC_ROWS, 3, L, WCO)

    for f in range(3):
        CO[:, f] = jnp.swapaxes(coarse_old[f], 0, 1)

    def fine_f(r):
        row = q * R + (r - HALO)
        return rotation * (2.0 * (row.astype(F32) + 0.5) / (R * NL) - 1.0), (row >= 0) & (row < R * NL)

    stages = (
        (YA, Y1, (0.0, 1.0), 1.0),
        (Y1, Y2, (0.75, 0.25), 0.25),
        (Y2, YA, (1.0 / 3.0, 2.0 / 3.0), 2.0 / 3.0),
    )

    def pressure(stage, pieces):
        src = stages[stage][0]
        count = sum(c for _, c in pieces)
        rows = [src[pl.ds(a, c), 0] for a, c in pieces]
        rows = rows[0] if len(rows) == 1 else jnp.concatenate(rows, axis=0)
        size = count * L
        result = mixed(KF[pl.ds(0, size), pl.ds(0, size)], rows.reshape(size, W)).reshape(count, L, W)
        at = 0
        for a, c in pieces:
            PB[stage, pl.ds(a, c)] = result[at:at + c]
            at += c

    def row_pressure(stage, r):
        e = stages[stage][0][r, 0]
        total = widened(CF[0], W) * e
        for shift in range(1, L):
            total = total + widened(CF[shift], W) * pltpu.roll(e, shift, axis=0)
        PB[stage, r] = total

    def fine_row(stage, r):
        src, dst, weights, g = stages[stage]
        f, inside = fine_f(r)
        new = updated(src, r, PB.at[stage], depth_of(W), WET[r], f, 1.0, YA, weights, g * time_step, inside)
        for i in range(3):
            dst[r, i] = new[i]

    def coarse_first():
        sums = jnp.stack([YA[1] + YA[2], YA[HALO + R] + YA[HALO + R + 1]])
        outer = (0.25 * picked(sums.reshape(-1, W), WR[...])).reshape(2, 3, L, WCO)
        C0[0] = outer[0]
        C0[RC_ROWS + 1] = outer[1]
        size = (RC_ROWS + 2) * L
        P0[...] = mixed(KC[pl.ds(0, size), pl.ds(0, size)], C0[:, 0].reshape(size, WCO)).reshape(RC_ROWS + 2, L, WCO)
        pairs = (iota((RC_ROWS, R), 1) // 2 == iota((RC_ROWS, R), 0)).astype(F32)
        wet_full = (jnp.dot(jnp.dot(pairs, wet_cells[...].astype(F32)), WR[...].astype(F32)) > 3.5).astype(F32)
        for i in range(RC_ROWS):
            W0[i] = jnp.broadcast_to(wet_full[i:i + 1, :], (L, WCO))

        @pl.loop(1, RC_ROWS + 1)
        def _(r):
            row = q * RC_ROWS + r - 1
            f = rotation * (2.0 * (row.astype(F32) + 0.5) / (RC_ROWS * NL) - 1.0)
            new = updated(C0, r, P0, depth_of(WCO), W0[r - 1], f, 2.0, None, (0.0, 1.0), STEPS * time_step, True)
            for i in range(3):
                CN[r - 1, i] = new[i]

    HU = RC_ROWS // 2
    lanes = iota((L, 128), 1)
    group = lanes // SLAB

    def side_by_side(parts):
        packed = parts[0]
        for g in range(1, 4):
            packed = jnp.where(group == g, parts[g], packed)
        return packed

    def own_result(source):
        return pltpu.make_async_copy(source, RC.at[n], in_sem.at[8])

    def first_result():
        return pltpu.make_async_copy(PK, RC, in_sem.at[8])

    def slot_of(unit):
        return {1: 0, 2: 1, 0: 2, 3: 3}[unit]

    def deltas(units):
        rows = [2 * unit + more for unit in units for more in range(2)]
        sums = jnp.stack([YA[HALO + 2 * i] + YA[HALO + 1 + 2 * i] for i in rows])
        change = (0.25 * picked(sums.reshape(-1, W), WW[...])).reshape(len(rows), 3, L, W)
        for at, i in enumerate(rows):
            DL[i] = change[at] + BW[pl.ds(i * 3 * L, 3 * L)].reshape(3, L, W)
        for i in units:
            for f in range(3):
                for j in range(NT // 2):
                    a = DL[2 * i, f, :, pl.ds(128 * j, 128)]
                    b = DL[2 * i + 1, f, :, pl.ds(128 * j, 128)]
                    TX[2 * j, slot_of(i), f] = jnp.where(lanes < 64, a, rolled(b, 64))
                    TX[2 * j + 1, slot_of(i), f] = jnp.where(lanes < 64, rolled(a, 64), b)

    def piece(d, phase, units):
        if d == 0 or units == 4:
            return 2 * phase, 2
        if phase == 1:
            return (3 if d == 1 else 2), 1
        return {1: (0, 0), 2: (1 if d == 1 else 0, 1), 3: (0, 2)}[units]

    def delta_copy(m, phase):
        return pltpu.make_async_remote_copy(
            src_ref=TX.at[m, pl.ds(2 * phase, 2)], dst_ref=RX.at[n, pl.ds(HU + 2 * phase, 2)],
            send_sem=tx_send.at[m, phase], recv_sem=rx_recv.at[n, phase],
            device_id=(m, q), device_id_type=MESH)

    def delta_arrival(s, phase):
        return pltpu.make_async_remote_copy(
            src_ref=TX.at[0, pl.ds(0, 2)], dst_ref=RX.at[s, pl.ds(HU + 2 * phase, 2)],
            send_sem=tx_send.at[0, phase], recv_sem=rx_recv.at[s, phase],
            device_id=(s, q), device_id_type=MESH)

    def for_deltas(phase, act):
        @pl.when(n < NT - 1)
        def _():
            @pl.loop(1, NT)
            def _(j):
                act(delta_copy(lax.rem(n + j, NT), phase))

    def send_deltas(phase):
        for_deltas(phase, lambda copy: copy.start())

        @pl.when(n < NT - 1)
        def _():
            RX[n, pl.ds(HU + 2 * phase, 2)] = TX[n, pl.ds(2 * phase, 2)]

    def passing(s, d, phase):
        first, count = piece(d, phase, (NT - s) // 2)
        side = 0 if d == 1 else 1
        return pltpu.make_async_remote_copy(
            src_ref=RX.at[s, pl.ds(HU + first, count)], dst_ref=RX.at[s, pl.ds(HU * (1 - d) + first, count)],
            send_sem=fw_send.at[s, side, phase], recv_sem=fw_recv.at[s, side, phase],
            device_id=(n, q + d), device_id_type=MESH)

    def passed_on(phase):
        return [(s, d, there) for s in range(NT - 1) for d, there in ((1, down), (-1, up))
                if piece(d, phase, (NT - s) // 2)[1]]

    def pass_deltas(phase):
        for s in range(NT - 1):
            @pl.when(n != s)
            def _(s=s):
                delta_arrival(s, phase).wait_recv()
            for t, d, there in passed_on(phase):
                if t == s:
                    @pl.when(there)
                    def _(s=s, d=d):
                        passing(s, d, phase).start()

    @pl.loop(0, STEPS)
    def _(k):
        for stage in range(3):
            pressure(stage, [(HALO + stage, R - 2 * stage)])

            for r in range(R - 2 * (stage + 1)):
                fine_row(stage, HALO + stage + 1 + r)

        @pl.when(k == STEPS - 1)
        def _():
            deltas((1, 2))
            send_deltas(0)

        for side in (-1, 1):
            slot = 0 if side == -1 else 1

            @pl.when(inside_side[side])
            def _(side=side, slot=slot):
                for j in range(HALO):
                    halo_arrival(k, side, j).wait_recv()
                YA[pl.ds(0 if side == -1 else HALO + R, HALO)] = HB[k, slot]
                for j in range(HALO):
                    halo_copy(k, side, j).wait_send()

        @pl.when(k == 0)
        def _():
            for side in (-1, 1):
                @pl.when(inside_side[side])
                def _(side=side):
                    wet_copy(side).wait_send()
                    wet_copy(-side).wait_recv()
            for r in range(HALO):
                WET[r] = jnp.broadcast_to(WX[0, R - HALO + r:R - HALO + r + 1, :].astype(F32), (L, W))
                WET[HALO + R + r] = jnp.broadcast_to(WX[1, r:r + 1, :].astype(F32), (L, W))

        for j in range(HALO):
            for stage in range(3):
                low, high = HALO - j + stage, HALO + R - 1 + j - stage
                row_pressure(stage, low - 1)
                row_pressure(stage, high + 1)
                fine_row(stage, low)
                fine_row(stage, high)

            @pl.when(k < STEPS - 1)
            def _(j=j):
                send_row(k + 1, j)

        @pl.when(k == 0)
        def _():
            @pl.when(n == 0)
            def _():
                coarse_first()
                for m in range(NT):
                    at = SLAB * m // 128 * 128
                    for b in range(2):
                        for i in range(3):
                            PK[m, b, i] = side_by_side([
                                rolled(CN[4 * b + g, i, :, pl.ds(at, 128)], SLAB * g - (SLAB * m - at)) for g in range(4)])
                first_result().start()
                BW[...] = picked((CN[...] - CO[...]).reshape(-1, WCO), W2[...])

            @pl.when(n > 0)
            def _():
                BW[...] = picked((-CO[...]).reshape(-1, WCO), W2[...])

    keep = pltpu.make_async_copy(YA.at[pl.ds(HALO, R)], ends, in_sem.at[5 + 2])
    keep.start()
    deltas((0, 3))
    @pl.when(n <= 2)
    def _():
        send_deltas(1)

    pass_deltas(0)

    @pl.when(n > 2)
    def _():
        send_deltas(1)


    E = 3 * RC_ROWS
    col = iota((W, 128), 1)
    own = (n * SLAB - 16 + col) & (WCO - 1)
    picks = jnp.where(((iota((W, 128), 0) >> 1) == own) & (col < 64), 1.0, 0.0).astype(F32)
    pairs = (iota((RC_ROWS, R), 1) // 2 == iota((RC_ROWS, R), 0)).astype(F32)
    for part, cells in enumerate((WX[0], wet_cells[...], WX[1])):
        window = (jnp.dot(jnp.dot(pairs, cells.astype(F32)), picks) > 3.5).astype(F32)
        for i in range(RC_ROWS):
            WC[part * RC_ROWS + i] = jnp.broadcast_to(window[i:i + 1, :], (L, 128))

    pass_deltas(1)

    def arrived(s):
        for phase in range(2):
            for t, d, _ in passed_on(phase):
                if t == s:
                    @pl.when(up if d == 1 else down)
                    def _(d=d, phase=phase):
                        passing(s, d, phase).wait_recv()

    def row_of(s, r, f):
        x = RX[s, r // 2 // HU * HU + slot_of(r // 2 % HU), f]
        return x if r % 2 == 0 else rolled(x, 64)

    arrived(0)
    for r in range(E):
        for f in range(3):
            CT[0, r, f] = row_of(0, r, f)

    def result_copy(s):
        return pltpu.make_async_remote_copy(
            src_ref=TC.at[s], dst_ref=RC.at[n], send_sem=tc_send.at[s], recv_sem=rc_recv.at[n],
            device_id=(s, q), device_id_type=MESH)

    def result_arrival(m):
        return pltpu.make_async_remote_copy(
            src_ref=TC.at[0], dst_ref=RC.at[m], send_sem=tc_send.at[0], recv_sem=rc_recv.at[m],
            device_id=(m, q), device_id_type=MESH)

    depth = depth_of(128)
    for s in range(1, NT):
        now, later = CT.at[(s - 1) % 2], CT.at[s % 2]
        h = NT - 1 - s
        lo, hi = RC_ROWS - h, 2 * RC_ROWS + h
        for r in range(lo - 1, hi + 1):
            e = now[r, 0]
            total = (0.5 * CF[0]) * e
            for shift in range(1, L):
                total = total + (0.5 * CF[shift]) * pltpu.roll(e, shift, axis=0)
            PC[r] = total
        for r in range(lo, hi):
            row = q * RC_ROWS + (r - RC_ROWS)
            f = rotation * (2.0 * (row.astype(F32) + 0.5) / (RC_ROWS * NL) - 1.0)
            inside = (row >= 0) & (row < RC_ROWS * NL)
            new = updated(now, r, PC, depth, WC[r], f, 2.0, None, (0.0, 1.0), STEPS * time_step, inside)
            for i in range(3):
                if RC_ROWS <= r < 2 * RC_ROWS:
                    RES[r - RC_ROWS, i] = new[i]
                if s < NT - 1:
                    later[r, i] = new[i]
        for b in range(2):
            for i in range(3):
                TC[s, b, i] = side_by_side([rolled(RES[4 * b + g, i], SLAB * g - 16) for g in range(4)])

        @pl.when(n != s)
        def _(s=s):
            result_copy(s).start()

        @pl.when(n == s)
        def _(s=s):
            own_result(TC.at[s]).start()

        if s < NT - 1:
            arrived(s)
            for r in range(lo, hi):
                for i in range(3):
                    later[r, i] = later[r, i] + row_of(s, r, i)

    @pl.when(n > 0)
    def _():
        @pl.loop(1, NT)
        def _(j):
            result_arrival(lax.rem(n + j, NT)).wait_recv()

        own_result(TC.at[n]).wait()

    @pl.when(n == 0)
    def _():
        first_result().wait()

    keep.wait()
    for phase in range(2):
        for_deltas(phase, lambda copy: copy.wait_send())
        for s, d, there in passed_on(phase):
            @pl.when(there)
            def _(s=s, d=d, phase=phase):
                passing(s, d, phase).wait_send()
    for s in range(1, NT):
        @pl.when(n != s)
        def _(s=s):
            result_copy(s).wait_send()


def correct(state_in, coarse_in, old_in, ends, result, S, N, O, E, Q, WP, in_sem, out_sem):
    R, _, L, W = S.shape
    C, WCO = R // 2, W // 2
    SLAB = WCO // N.shape[0]
    group = iota((L, 128), 1) // SLAB
    fetches = []
    for f in range(3):
        for i, (source, target) in enumerate(((coarse_in.at[:, :, f], N.at[:, :, f]), (old_in.at[f], O.at[f]),
                                              (state_in.at[:, f], S.at[:, f]))):
            fetches.append(pltpu.make_async_copy(source, target, in_sem.at[f, i]))
            fetches[-1].start()
    WP[...] = jnp.where((iota((WCO, W), 1) >> 1) == iota((WCO, W), 0), 1.0, 0.0).astype(jnp.bfloat16)
    stores = []
    for f in range(3):
        fetches[3 * f].wait()
        fetches[3 * f + 1].wait()
        rows = []
        for r in range(C):
            parts = []
            for j in range(WCO // 128):
                value = rolled(N[4 * j, r // 4, f], -SLAB * (r % 4))
                for m in range(1, 4):
                    value = jnp.where(group == m, rolled(N[4 * j + m, r // 4, f], SLAB * (m - r % 4)), value)
                parts.append(value)
            rows.append(jnp.concatenate(parts, axis=1))
        new = jnp.stack(rows)
        Q[f] = jnp.swapaxes(new, 0, 1)
        change = new - jnp.swapaxes(O[f], 0, 1)
        change = picked(change.reshape(C * L, WCO), WP[...]).reshape(C, L, W)
        fetches[3 * f + 2].wait()
        for b in range(R // 8):
            rows = jnp.stack([S[8 * b + i, f] + change[4 * b + i // 2] for i in range(8)])
            E[f, :, pl.ds(8 * b, 8), :] = jnp.swapaxes(rows, 0, 1)
        for i, (source, target) in enumerate(((E.at[f], ends.at[f]), (Q.at[f], result.at[f]))):
            stores.append(pltpu.make_async_copy(source, target, out_sem.at[f, i]))
            stores[-1].start()
    for store in stores:
        store.wait()


def local(NT, NL, starts, coarse_old, mean_depth, coupling, wet_cells):
    R, W = wet_cells.shape
    L = 8
    C, WCO = R // 2, W // 2
    E = R + 2 * HALO
    vmem = lambda *shape: pltpu.VMEM(shape, F32)
    half = lambda *shape: pltpu.VMEM(shape, jnp.bfloat16)
    sems = lambda *shape: pltpu.SemaphoreType.DMA(shape)
    far = pl.BlockSpec(memory_space=pltpu.HBM)
    state, coarse_new = pl.pallas_call(
        functools.partial(kernel, NT, NL),
        out_shape=(jax.ShapeDtypeStruct((R, 3, L, W), F32), jax.ShapeDtypeStruct((NT, 2, 3, L, 128), F32)),
        in_specs=[far] * 5,
        out_specs=(far, far),
        scratch_shapes=[
            vmem(3, L, R, W), vmem(3, L, C, WCO), vmem(L, L), pltpu.VMEM((R, W), jnp.int32), pltpu.SMEM((L,), F32),
            vmem(L, 128), vmem(L, L, 128), sems(9),
            vmem(E, 3, L, W), vmem(E, 3, L, W), vmem(E, 3, L, W), vmem(3, E, L, W), vmem(E, L, W),
            pltpu.VMEM((2, R, W), jnp.int32), vmem(STEPS, 2, HALO, 3, L, W),
            vmem(3 * C * L, 3 * C * L), vmem(3 * C * L, 3 * C * L),
            half(W, W), half(WCO, W), half(W, WCO), vmem(C, 3, L, W),
            vmem(NT, C // 2, 3, L, 128), vmem(NT - 1, 3 * C // 2, 3, L, 128),
            vmem(NT, 2, 3, L, 128), vmem(NT, 2, 3, L, 128),
            vmem(2, 3 * C, 3, L, 128), vmem(3 * C, L, 128), vmem(3 * C, L, 128), vmem(C, 3, L, 128),
            vmem(C, 3, L, WCO), vmem(C * 3 * L, W), vmem(C, 3, L, WCO),
            vmem(C + 2, 3, L, WCO), vmem(C + 2, L, WCO), vmem(C, L, WCO),
            sems(STEPS, 2, HALO), sems(STEPS, 2, HALO), sems(2), sems(2), sems(NT, 2), sems(NT - 1, 2), sems(NT - 1, 2, 2), sems(NT - 1, 2, 2), sems(NT), sems(NT),
        ],
        compiler_params=pltpu.CompilerParams(
            collective_id=0, has_side_effects=True, vmem_limit_bytes=63 * 1024 * 1024),
    )(starts[0], coarse_old[0], mean_depth, coupling, wet_cells)
    ends, result = pl.pallas_call(
        correct,
        out_shape=(jax.ShapeDtypeStruct((3, L, R, W), F32), jax.ShapeDtypeStruct((3, L, C, WCO), F32)),
        in_specs=[far] * 3,
        out_specs=(far, far),
        scratch_shapes=[
            vmem(R, 3, L, W), vmem(NT, 2, 3, L, 128), vmem(3, L, C, WCO), vmem(3, L, R, W), vmem(3, L, C, WCO),
            half(WCO, W), sems(3, 3), sems(3, 2)],
        compiler_params=pltpu.CompilerParams(vmem_limit_bytes=63 * 1024 * 1024),
    )(state, coarse_new, coarse_old[0])
    return ends[None], result[None]


def solution(mesh):
    NT, NL = mesh.shape["tm"], mesh.shape["lat"]
    in_specs = (
        P("tm", None, None, "lat", None),
        P("tm", None, None, "lat", None),
        P(),
        P(),
        P("lat", None),
    )
    out_specs = (P("tm", None, None, "lat", None), P("tm", None, None, "lat", None))
    return jax.shard_map(functools.partial(local, NT, NL), mesh=mesh, in_specs=in_specs, out_specs=out_specs,
                         check_vma=False)
```

```python
import functools

import jax
import jax.numpy as jnp
from jax import lax
from jax.experimental import pallas as pl
from jax.experimental.pallas import tpu as pltpu
from jax.sharding import PartitionSpec as P

MESH = pl.DeviceIdType.MESH
F32 = jnp.float32

STEPS = 4
time_step = 0.15
viscosity = 0.02
rotation = 0.3

HALO = 3


def iota(shape, dim):
    return lax.broadcasted_iota(jnp.int32, shape, dim)


def dot(a, b):
    return jnp.dot(a, b, precision=lax.Precision.HIGHEST, preferred_element_type=F32)


def split(x, terms):
    parts = []
    for _ in range(terms):
        part = x.astype(jnp.bfloat16)
        parts.append(part)
        x = x - part.astype(F32)
    return parts


def picked(x, selector):
    rows = x.shape[0]
    result = jnp.dot(jnp.concatenate(split(x, 3), axis=0), selector, preferred_element_type=F32)
    return result[:rows] + (result[rows:2 * rows] + result[2 * rows:])


def mixed(matrix, x):
    high, low = split(matrix, 2)
    x_high, x_low = split(x, 2)
    product = lambda a, b: jnp.dot(a, b, preferred_element_type=F32)
    return product(high, x_high) + (product(high, x_low) + product(low, x_high))


def widened(x, width):
    return x if width == x.shape[1] else jnp.concatenate([x] * (width // x.shape[1]), axis=1)


def rolled(x, shift):
    return pltpu.roll(x, shift % x.shape[-1], axis=x.ndim - 1)


def updated(src, r, p, depth, wet, f, spacing, old, weights, step, inside):
    k = viscosity / (spacing * spacing)
    half = 0.5 / spacing
    e, u, v = src[r, 0], src[r, 1], src[r, 2]
    un, us = src[r + 1, 1], src[r - 1, 1]
    vn, vs = src[r + 1, 2], src[r - 1, 2]
    hvn = (depth + src[r + 1, 0]) * vn
    hvs = (depth + src[r - 1, 0]) * vs
    hu = (depth + e) * u
    pc = p[r]
    ue, uw = rolled(u, -1), rolled(u, 1)
    ve, vw = rolled(v, -1), rolled(v, 1)
    u2, v2 = u * half, v * half
    east, west, north, south = k - u2, k + u2, k - v2, k + v2
    zu = (ue * east + uw * west) + (un * north + us * south)
    zv = (ve * east + vw * west) + (vn * north + vs * south)
    zu = zu + (f * v - (4.0 * k) * u) - (rolled(pc, -1) - rolled(pc, 1))
    zv = zv - (f * u + (4.0 * k) * v) - (p[r + 1] - p[r - 1])
    ze = (rolled(hu, -1) - rolled(hu, 1)) + (hvn - hvs)
    w = wet * step
    ce = jnp.where(inside, -step * half, 0.0).astype(F32)
    out = [ce * ze, w * zu, w * zv]
    first, second = weights
    now = [e, u, v]
    for i in range(3):
        out[i] = out[i] + (now[i] if second == 1.0 else second * now[i])
        if first != 0.0:
            out[i] = out[i] + first * old[r, i]
    return out


def kernel(NT, NL, starts_in, old_in, depth_in, coupling_in, wet_in, ends, RC,
           SV, OV, CV, WV, DS, DP, CF, in_sem, YA, Y1, Y2, PB, WET, WX, HB, KF, KC, WW, W2, WR, DL, TX, RX, TC, PK, CT, PC, WC, RES,
           CO, BW, CN, C0, P0, W0,
           hs_send, hs_recv, wx_send, wx_recv, tx_send, rx_recv, fw_send, fw_recv, tc_send, rc_recv):
    starts, coarse_old, mean_depth, coupling, wet_cells = SV, OV, DS, CV, WV
    R, W = wet_cells.shape
    L = 8
    fetches = [pltpu.make_async_copy(source, target, in_sem.at[i]) for i, (source, target) in enumerate(
        [(starts_in.at[f], SV.at[f]) for f in range(3)] + [(wet_in, WV), (coupling_in, CV), (depth_in, DS), (old_in, OV)])]
    for fetch in fetches:
        fetch.start()
    RC_ROWS, WCO = R // 2, W // 2
    SLAB = WCO // NT
    n, q = lax.axis_index("tm"), lax.axis_index("lat")
    up, down = q > 0, q < NL - 1
    inside_side = {-1: up, 1: down}

    barrier = pltpu.get_barrier_semaphore()

    def greet(m, row):
        pl.semaphore_signal(barrier, inc=1, device_id=(m, row), device_id_type=MESH)

    for j in range(1, NT):
        greet(lax.rem(n + j, NT), q)
    for d in (-1, 1):
        @pl.when(inside_side[d])
        def _(d=d):
            greet(n, q + d)

    pl.semaphore_wait(barrier, (NT - 1) + up.astype(jnp.int32) + down.astype(jnp.int32))
    for f in range(3):
        fetches[f].wait()
        for b in range(R // 8):
            YA[pl.ds(HALO + 8 * b, 8), f] = jnp.swapaxes(starts[f, :, pl.ds(8 * b, 8), :], 0, 1)
        for side in (-1, 1):
            @pl.when(inside_side[side])
            def _(f=f, side=side):
                slot = 1 if side == -1 else 0
                pltpu.make_async_remote_copy(
                    src_ref=YA.at[pl.ds(HALO if side == -1 else R, HALO), f], dst_ref=HB.at[0, slot, :, f],
                    send_sem=hs_send.at[0, slot, f], recv_sem=hs_recv.at[0, slot, f],
                    device_id=(n, q + side), device_id_type=MESH).start()


    def halo_copy(k, side, j):
        row = HALO + HALO - 1 - j if side == -1 else R + j
        slot = 1 if side == -1 else 0
        return pltpu.make_async_remote_copy(
            src_ref=YA.at[row], dst_ref=HB.at[k, slot, row - HALO if side == -1 else j],
            send_sem=hs_send.at[k, slot, j], recv_sem=hs_recv.at[k, slot, j],
            device_id=(n, q + side), device_id_type=MESH)

    def halo_arrival(k, side, j):
        slot = 0 if side == -1 else 1
        return pltpu.make_async_remote_copy(
            src_ref=YA.at[0], dst_ref=HB.at[k, slot, j if side == -1 else HALO - 1 - j],
            send_sem=hs_send.at[k, slot, j], recv_sem=hs_recv.at[k, slot, j],
            device_id=(n, q + side), device_id_type=MESH)

    def wet_copy(side):
        slot = 1 if side == -1 else 0
        return pltpu.make_async_remote_copy(
            src_ref=wet_cells, dst_ref=WX.at[slot], send_sem=wx_send.at[slot], recv_sem=wx_recv.at[slot],
            device_id=(n, q + side), device_id_type=MESH)

    def send_row(k, j):
        for side in (-1, 1):
            @pl.when(inside_side[side])
            def _(side=side):
                halo_copy(k, side, j).start()

    for fetch in fetches[3:]:
        fetch.wait()
    for side in (-1, 1):
        @pl.when(inside_side[side])
        def _(side=side):
            wet_copy(side).start()

        @pl.when(jnp.logical_not(inside_side[side]))
        def _(side=side):
            slot = 0 if side == -1 else 1
            WX[slot] = jnp.zeros((R, W), jnp.int32)
            YA[pl.ds(0 if side == -1 else HALO + R, HALO)] = jnp.zeros((HALO, 3, L, W), F32)
            RX[:, pl.ds(0 if side == -1 else RC_ROWS, RC_ROWS // 2)] = jnp.zeros(
                (NT - 1, RC_ROWS // 2, 3, L, 128), F32)

    KN = KF.shape[0]
    spread = (iota((KN, L), 0) % L == iota((KN, L), 1)).astype(F32)
    spread_t = (iota((L, KN), 1) % L == iota((L, KN), 0)).astype(F32)
    blocks = dot(dot(spread, coupling[...]), spread_t)
    blocks = jnp.where(iota((KN, KN), 0) // L == iota((KN, KN), 1) // L, blocks, 0.0)
    KF[...] = 0.5 * blocks
    KC[...] = 0.25 * blocks
    for shift in range(L):
        column = (iota((L, L), 0) - shift + L) & (L - 1)
        part = jnp.sum(jnp.where(iota((L, L), 1) == column, coupling[...], 0.0), axis=1, keepdims=True)
        CF[shift] = jnp.broadcast_to(0.5 * part, (L, 128))

    layer = iota((L, 128), 0)
    value = jnp.zeros((L, 128), F32)
    for l in range(L):
        value = jnp.where(layer == l, mean_depth[l], value)
    DP[...] = value

    def depth_of(width):
        return widened(DP[...], width)

    wet_own = wet_cells[...].astype(F32)
    for r in range(R):
        WET[HALO + r] = jnp.broadcast_to(wet_own[r:r + 1, :], (L, W))

    position = iota((8, W), 1)
    target = ((position >> 6) * SLAB - 16 + (position & 63)) & (WCO - 1)
    target = target[:1]
    selector = lambda where: jnp.where(where, 1.0, 0.0).astype(jnp.bfloat16)
    WW[...] = selector((iota((W, W), 0) >> 1) == target)
    W2[...] = selector(iota((WCO, W), 0) == target)
    WR[...] = selector((iota((W, WCO), 0) >> 1) == iota((W, WCO), 1))

    @pl.when(n == 0)
    def _():
        sums = jnp.stack([YA[HALO + 2 * i] + YA[HALO + 1 + 2 * i] for i in range(RC_ROWS)])
        C0[pl.ds(1, RC_ROWS)] = (0.25 * picked(sums.reshape(-1, W), WR[...])).reshape(RC_ROWS, 3, L, WCO)

    for f in range(3):
        CO[:, f] = jnp.swapaxes(coarse_old[f], 0, 1)

    def fine_f(r):
        row = q * R + (r - HALO)
        return rotation * (2.0 * (row.astype(F32) + 0.5) / (R * NL) - 1.0), (row >= 0) & (row < R * NL)

    stages = (
        (YA, Y1, (0.0, 1.0), 1.0),
        (Y1, Y2, (0.75, 0.25), 0.25),
        (Y2, YA, (1.0 / 3.0, 2.0 / 3.0), 2.0 / 3.0),
    )

    def pressure(stage, pieces):
        src = stages[stage][0]
        count = sum(c for _, c in pieces)
        rows = [src[pl.ds(a, c), 0] for a, c in pieces]
        rows = rows[0] if len(rows) == 1 else jnp.concatenate(rows, axis=0)
        size = count * L
        result = mixed(KF[pl.ds(0, size), pl.ds(0, size)], rows.reshape(size, W)).reshape(count, L, W)
        at = 0
        for a, c in pieces:
            PB[stage, pl.ds(a, c)] = result[at:at + c]
            at += c

    def row_pressure(stage, r):
        e = stages[stage][0][r, 0]
        total = widened(CF[0], W) * e
        for shift in range(1, L):
            total = total + widened(CF[shift], W) * pltpu.roll(e, shift, axis=0)
        PB[stage, r] = total

    def fine_row(stage, r):
        src, dst, weights, g = stages[stage]
        f, inside = fine_f(r)
        new = updated(src, r, PB.at[stage], depth_of(W), WET[r], f, 1.0, YA, weights, g * time_step, inside)
        for i in range(3):
            dst[r, i] = new[i]

    def coarse_first():
        sums = jnp.stack([YA[1] + YA[2], YA[HALO + R] + YA[HALO + R + 1]])
        outer = (0.25 * picked(sums.reshape(-1, W), WR[...])).reshape(2, 3, L, WCO)
        C0[0] = outer[0]
        C0[RC_ROWS + 1] = outer[1]
        size = (RC_ROWS + 2) * L
        P0[...] = mixed(KC[pl.ds(0, size), pl.ds(0, size)], C0[:, 0].reshape(size, WCO)).reshape(RC_ROWS + 2, L, WCO)
        pairs = (iota((RC_ROWS, R), 1) // 2 == iota((RC_ROWS, R), 0)).astype(F32)
        wet_full = (jnp.dot(jnp.dot(pairs, wet_cells[...].astype(F32)), WR[...].astype(F32)) > 3.5).astype(F32)
        for i in range(RC_ROWS):
            W0[i] = jnp.broadcast_to(wet_full[i:i + 1, :], (L, WCO))

        @pl.loop(1, RC_ROWS + 1)
        def _(r):
            row = q * RC_ROWS + r - 1
            f = rotation * (2.0 * (row.astype(F32) + 0.5) / (RC_ROWS * NL) - 1.0)
            new = updated(C0, r, P0, depth_of(WCO), W0[r - 1], f, 2.0, None, (0.0, 1.0), STEPS * time_step, True)
            for i in range(3):
                CN[r - 1, i] = new[i]

    HU = RC_ROWS // 2
    lanes = iota((L, 128), 1)
    group = lanes // SLAB

    def side_by_side(parts):
        packed = parts[0]
        for g in range(1, 4):
            packed = jnp.where(group == g, parts[g], packed)
        return packed

    def own_result(source):
        return pltpu.make_async_copy(source, RC.at[n], in_sem.at[8])

    def first_result():
        return pltpu.make_async_copy(PK, RC, in_sem.at[8])

    def slot_of(unit):
        return {1: 0, 2: 1, 0: 2, 3: 3}[unit]

    def deltas(units):
        rows = [2 * unit + more for unit in units for more in range(2)]
        sums = jnp.stack([YA[HALO + 2 * i] + YA[HALO + 1 + 2 * i] for i in rows])
        change = (0.25 * picked(sums.reshape(-1, W), WW[...])).reshape(len(rows), 3, L, W)
        for at, i in enumerate(rows):
            DL[i] = change[at] + BW[pl.ds(i * 3 * L, 3 * L)].reshape(3, L, W)
        for i in units:
            for f in range(3):
                for j in range(NT // 2):
                    a = DL[2 * i, f, :, pl.ds(128 * j, 128)]
                    b = DL[2 * i + 1, f, :, pl.ds(128 * j, 128)]
                    TX[2 * j, slot_of(i), f] = jnp.where(lanes < 64, a, rolled(b, 64))
                    TX[2 * j + 1, slot_of(i), f] = jnp.where(lanes < 64, rolled(a, 64), b)

    def piece(d, phase, units):
        if d == 0 or units == 4:
            return 2 * phase, 2
        if phase == 1:
            return (3 if d == 1 else 2), 1
        return {1: (0, 0), 2: (1 if d == 1 else 0, 1), 3: (0, 2)}[units]

    def delta_copy(m, phase):
        return pltpu.make_async_remote_copy(
            src_ref=TX.at[m, pl.ds(2 * phase, 2)], dst_ref=RX.at[n, pl.ds(HU + 2 * phase, 2)],
            send_sem=tx_send.at[m, phase], recv_sem=rx_recv.at[n, phase],
            device_id=(m, q), device_id_type=MESH)

    def delta_arrival(s, phase):
        return pltpu.make_async_remote_copy(
            src_ref=TX.at[0, pl.ds(0, 2)], dst_ref=RX.at[s, pl.ds(HU + 2 * phase, 2)],
            send_sem=tx_send.at[0, phase], recv_sem=rx_recv.at[s, phase],
            device_id=(s, q), device_id_type=MESH)

    def for_deltas(phase, act):
        @pl.when(n < NT - 1)
        def _():
            @pl.loop(1, NT)
            def _(j):
                act(delta_copy(lax.rem(n + j, NT), phase))

    def send_deltas(phase):
        for_deltas(phase, lambda copy: copy.start())

        @pl.when(n < NT - 1)
        def _():
            RX[n, pl.ds(HU + 2 * phase, 2)] = TX[n, pl.ds(2 * phase, 2)]

    def passing(s, d, phase):
        first, count = piece(d, phase, (NT - s) // 2)
        side = 0 if d == 1 else 1
        return pltpu.make_async_remote_copy(
            src_ref=RX.at[s, pl.ds(HU + first, count)], dst_ref=RX.at[s, pl.ds(HU * (1 - d) + first, count)],
            send_sem=fw_send.at[s, side, phase], recv_sem=fw_recv.at[s, side, phase],
            device_id=(n, q + d), device_id_type=MESH)

    def passed_on(phase):
        return [(s, d, there) for s in range(NT - 1) for d, there in ((1, down), (-1, up))
                if piece(d, phase, (NT - s) // 2)[1]]

    def pass_deltas(phase):
        for s in range(NT - 1):
            @pl.when(n != s)
            def _(s=s):
                delta_arrival(s, phase).wait_recv()
            for t, d, there in passed_on(phase):
                if t == s:
                    @pl.when(there)
                    def _(s=s, d=d):
                        passing(s, d, phase).start()

    @pl.loop(0, STEPS)
    def _(k):
        for stage in range(3):
            pressure(stage, [(HALO + stage, R - 2 * stage)])

            for r in range(R - 2 * (stage + 1)):
                fine_row(stage, HALO + stage + 1 + r)

        @pl.when(k == STEPS - 1)
        def _():
            deltas((1, 2))
            send_deltas(0)

        for side in (-1, 1):
            slot = 0 if side == -1 else 1

            @pl.when(inside_side[side])
            def _(side=side, slot=slot):
                for j in range(HALO):
                    halo_arrival(k, side, j).wait_recv()
                YA[pl.ds(0 if side == -1 else HALO + R, HALO)] = HB[k, slot]
                for j in range(HALO):
                    halo_copy(k, side, j).wait_send()

        @pl.when(k == 0)
        def _():
            for side in (-1, 1):
                @pl.when(inside_side[side])
                def _(side=side):
                    wet_copy(side).wait_send()
                    wet_copy(-side).wait_recv()
            for r in range(HALO):
                WET[r] = jnp.broadcast_to(WX[0, R - HALO + r:R - HALO + r + 1, :].astype(F32), (L, W))
                WET[HALO + R + r] = jnp.broadcast_to(WX[1, r:r + 1, :].astype(F32), (L, W))

        for j in range(HALO):
            for stage in range(3):
                low, high = HALO - j + stage, HALO + R - 1 + j - stage
                row_pressure(stage, low - 1)
                row_pressure(stage, high + 1)
                fine_row(stage, low)
                fine_row(stage, high)

            @pl.when(k < STEPS - 1)
            def _(j=j):
                send_row(k + 1, j)

        @pl.when(k == 0)
        def _():
            @pl.when(n == 0)
            def _():
                coarse_first()
                for m in range(NT):
                    at = SLAB * m // 128 * 128
                    for b in range(2):
                        for i in range(3):
                            PK[m, b, i] = side_by_side([
                                rolled(CN[4 * b + g, i, :, pl.ds(at, 128)], SLAB * g - (SLAB * m - at)) for g in range(4)])
                first_result().start()
                BW[...] = picked((CN[...] - CO[...]).reshape(-1, WCO), W2[...])

            @pl.when(n > 0)
            def _():
                BW[...] = picked((-CO[...]).reshape(-1, WCO), W2[...])

    keep = pltpu.make_async_copy(YA.at[pl.ds(HALO, R)], ends, in_sem.at[5 + 2])
    deltas((0, 3))
    @pl.when(n <= 2)
    def _():
        send_deltas(1)

    pass_deltas(0)

    @pl.when(n > 2)
    def _():
        send_deltas(1)


    E = 3 * RC_ROWS
    col = iota((W, 128), 1)
    own = (n * SLAB - 16 + col) & (WCO - 1)
    picks = jnp.where(((iota((W, 128), 0) >> 1) == own) & (col < 64), 1.0, 0.0).astype(F32)
    pairs = (iota((RC_ROWS, R), 1) // 2 == iota((RC_ROWS, R), 0)).astype(F32)
    for part, cells in enumerate((WX[0], wet_cells[...], WX[1])):
        window = (jnp.dot(jnp.dot(pairs, cells.astype(F32)), picks) > 3.5).astype(F32)
        for i in range(RC_ROWS):
            WC[part * RC_ROWS + i] = jnp.broadcast_to(window[i:i + 1, :], (L, 128))

    pass_deltas(1)
    keep.start()

    def arrived(s):
        for phase in range(2):
            for t, d, _ in passed_on(phase):
                if t == s:
                    @pl.when(up if d == 1 else down)
                    def _(d=d, phase=phase):
                        passing(s, d, phase).wait_recv()

    def row_of(s, r, f):
        x = RX[s, r // 2 // HU * HU + slot_of(r // 2 % HU), f]
        return x if r % 2 == 0 else rolled(x, 64)

    arrived(0)
    for r in range(E):
        for f in range(3):
            CT[0, r, f] = row_of(0, r, f)

    def result_copy(s):
        return pltpu.make_async_remote_copy(
            src_ref=TC.at[s], dst_ref=RC.at[n], send_sem=tc_send.at[s], recv_sem=rc_recv.at[n],
            device_id=(s, q), device_id_type=MESH)

    def result_arrival(m):
        return pltpu.make_async_remote_copy(
            src_ref=TC.at[0], dst_ref=RC.at[m], send_sem=tc_send.at[0], recv_sem=rc_recv.at[m],
            device_id=(m, q), device_id_type=MESH)

    depth = depth_of(128)
    for s in range(1, NT):
        now, later = CT.at[(s - 1) % 2], CT.at[s % 2]
        h = NT - 1 - s
        lo, hi = RC_ROWS - h, 2 * RC_ROWS + h
        for r in range(lo - 1, hi + 1):
            e = now[r, 0]
            total = (0.5 * CF[0]) * e
            for shift in range(1, L):
                total = total + (0.5 * CF[shift]) * pltpu.roll(e, shift, axis=0)
            PC[r] = total
        for r in range(lo, hi):
            row = q * RC_ROWS + (r - RC_ROWS)
            f = rotation * (2.0 * (row.astype(F32) + 0.5) / (RC_ROWS * NL) - 1.0)
            inside = (row >= 0) & (row < RC_ROWS * NL)
            new = updated(now, r, PC, depth, WC[r], f, 2.0, None, (0.0, 1.0), STEPS * time_step, inside)
            for i in range(3):
                if RC_ROWS <= r < 2 * RC_ROWS:
                    RES[r - RC_ROWS, i] = new[i]
                if s < NT - 1:
                    later[r, i] = new[i]
        for b in range(2):
            for i in range(3):
                TC[s, b, i] = side_by_side([rolled(RES[4 * b + g, i], SLAB * g - 16) for g in range(4)])

        @pl.when(n != s)
        def _(s=s):
            result_copy(s).start()

        @pl.when(n == s)
        def _(s=s):
            own_result(TC.at[s]).start()

        if s < NT - 1:
            arrived(s)
            for r in range(lo, hi):
                for i in range(3):
                    later[r, i] = later[r, i] + row_of(s, r, i)

    @pl.when(n > 0)
    def _():
        @pl.loop(1, NT)
        def _(j):
            result_arrival(lax.rem(n + j, NT)).wait_recv()

        own_result(TC.at[n]).wait()

    @pl.when(n == 0)
    def _():
        first_result().wait()

    keep.wait()
    for phase in range(2):
        for_deltas(phase, lambda copy: copy.wait_send())
        for s, d, there in passed_on(phase):
            @pl.when(there)
            def _(s=s, d=d, phase=phase):
                passing(s, d, phase).wait_send()
    for s in range(1, NT):
        @pl.when(n != s)
        def _(s=s):
            result_copy(s).wait_send()


def correct(state_in, coarse_in, old_in, ends, result, S, N, O, E, Q, WP, in_sem, out_sem):
    R, _, L, W = S.shape
    C, WCO = R // 2, W // 2
    SLAB = WCO // N.shape[0]
    group = iota((L, 128), 1) // SLAB
    fetches = []
    for f in range(3):
        for i, (source, target) in enumerate(((coarse_in.at[:, :, f], N.at[:, :, f]), (old_in.at[f], O.at[f]),
                                              (state_in.at[:, f], S.at[:, f]))):
            fetches.append(pltpu.make_async_copy(source, target, in_sem.at[f, i]))
            fetches[-1].start()
    WP[...] = jnp.where((iota((WCO, W), 1) >> 1) == iota((WCO, W), 0), 1.0, 0.0).astype(jnp.bfloat16)
    stores = []
    for f in range(3):
        fetches[3 * f].wait()
        fetches[3 * f + 1].wait()
        rows = []
        for r in range(C):
            parts = []
            for j in range(WCO // 128):
                value = rolled(N[4 * j, r // 4, f], -SLAB * (r % 4))
                for m in range(1, 4):
                    value = jnp.where(group == m, rolled(N[4 * j + m, r // 4, f], SLAB * (m - r % 4)), value)
                parts.append(value)
            rows.append(jnp.concatenate(parts, axis=1))
        new = jnp.stack(rows)
        Q[f] = jnp.swapaxes(new, 0, 1)
        change = new - jnp.swapaxes(O[f], 0, 1)
        change = picked(change.reshape(C * L, WCO), WP[...]).reshape(C, L, W)
        fetches[3 * f + 2].wait()
        for b in range(R // 8):
            rows = jnp.stack([S[8 * b + i, f] + change[4 * b + i // 2] for i in range(8)])
            E[f, :, pl.ds(8 * b, 8), :] = jnp.swapaxes(rows, 0, 1)
        for i, (source, target) in enumerate(((E.at[f], ends.at[f]), (Q.at[f], result.at[f]))):
            stores.append(pltpu.make_async_copy(source, target, out_sem.at[f, i]))
            stores[-1].start()
    for store in stores:
        store.wait()


def local(NT, NL, starts, coarse_old, mean_depth, coupling, wet_cells):
    R, W = wet_cells.shape
    L = 8
    C, WCO = R // 2, W // 2
    E = R + 2 * HALO
    vmem = lambda *shape: pltpu.VMEM(shape, F32)
    half = lambda *shape: pltpu.VMEM(shape, jnp.bfloat16)
    sems = lambda *shape: pltpu.SemaphoreType.DMA(shape)
    far = pl.BlockSpec(memory_space=pltpu.HBM)
    state, coarse_new = pl.pallas_call(
        functools.partial(kernel, NT, NL),
        out_shape=(jax.ShapeDtypeStruct((R, 3, L, W), F32), jax.ShapeDtypeStruct((NT, 2, 3, L, 128), F32)),
        in_specs=[far] * 5,
        out_specs=(far, far),
        scratch_shapes=[
            vmem(3, L, R, W), vmem(3, L, C, WCO), vmem(L, L), pltpu.VMEM((R, W), jnp.int32), pltpu.SMEM((L,), F32),
            vmem(L, 128), vmem(L, L, 128), sems(9),
            vmem(E, 3, L, W), vmem(E, 3, L, W), vmem(E, 3, L, W), vmem(3, E, L, W), vmem(E, L, W),
            pltpu.VMEM((2, R, W), jnp.int32), vmem(STEPS, 2, HALO, 3, L, W),
            vmem(3 * C * L, 3 * C * L), vmem(3 * C * L, 3 * C * L),
            half(W, W), half(WCO, W), half(W, WCO), vmem(C, 3, L, W),
            vmem(NT, C // 2, 3, L, 128), vmem(NT - 1, 3 * C // 2, 3, L, 128),
            vmem(NT, 2, 3, L, 128), vmem(NT, 2, 3, L, 128),
            vmem(2, 3 * C, 3, L, 128), vmem(3 * C, L, 128), vmem(3 * C, L, 128), vmem(C, 3, L, 128),
            vmem(C, 3, L, WCO), vmem(C * 3 * L, W), vmem(C, 3, L, WCO),
            vmem(C + 2, 3, L, WCO), vmem(C + 2, L, WCO), vmem(C, L, WCO),
            sems(STEPS, 2, HALO), sems(STEPS, 2, HALO), sems(2), sems(2), sems(NT, 2), sems(NT - 1, 2), sems(NT - 1, 2, 2), sems(NT - 1, 2, 2), sems(NT), sems(NT),
        ],
        compiler_params=pltpu.CompilerParams(
            collective_id=0, has_side_effects=True, vmem_limit_bytes=63 * 1024 * 1024),
    )(starts[0], coarse_old[0], mean_depth, coupling, wet_cells)
    ends, result = pl.pallas_call(
        correct,
        out_shape=(jax.ShapeDtypeStruct((3, L, R, W), F32), jax.ShapeDtypeStruct((3, L, C, WCO), F32)),
        in_specs=[far] * 3,
        out_specs=(far, far),
        scratch_shapes=[
            vmem(R, 3, L, W), vmem(NT, 2, 3, L, 128), vmem(3, L, C, WCO), vmem(3, L, R, W), vmem(3, L, C, WCO),
            half(WCO, W), sems(3, 3), sems(3, 2)],
        compiler_params=pltpu.CompilerParams(vmem_limit_bytes=63 * 1024 * 1024),
    )(state, coarse_new, coarse_old[0])
    return ends[None], result[None]


def solution(mesh):
    NT, NL = mesh.shape["tm"], mesh.shape["lat"]
    in_specs = (
        P("tm", None, None, "lat", None),
        P("tm", None, None, "lat", None),
        P(),
        P(),
        P("lat", None),
    )
    out_specs = (P("tm", None, None, "lat", None), P("tm", None, None, "lat", None))
    return jax.shard_map(functools.partial(local, NT, NL), mesh=mesh, in_specs=in_specs, out_specs=out_specs,
                         check_vma=False)
```
